32 devices in a mesh: tm: 8 (over z, x), feat: 2 (over core), rep: 2 (over y).
Axes of the slice: x: 2, y: 2, z: 4, core: 2. Of those that a mesh axis runs over, the one named last changes fastest.
Arguments:
- frames: bfloat16 [2, 2048, 16384], P('rep', 'tm', 'feat'), may hold values from -50 to 50, as said below
- panel_low: bfloat16 [16384, 512], P('feat', 'tm'), may hold values from -0.046875 to 0.046875
- panel_high: bfloat16 [16384, 512], P('feat', 'tm'), may hold values from -0.046875 to 0.046875
- lags: int32 [2], P('rep'), may hold values from 1 to 64, as said below
- seg_lengths: int32 [2, 64], P('rep'), may hold values from 1 to 256, 2048 in all within a row
- ridge: float32 [32], replicated, may hold values from 0.01 to 10
Outputs:
- covariances: float32 [3, 1024, 1024], P(None, ('tm', 'feat', 'rep'))
- scores: float32 [1024, 32], P(('tm', 'feat', 'rep'))
The draws below stay inside these ranges and needn't reach their ends.
Inputs may be any that keep to these rules, and one draw needn't show every extreme that they name: The frames of each run follow one trajectory in time. `lags`: one run has the lag 64. `seg_lengths`: each row sums to 2048.
All inputs are finite; a program needn't handle non-finite values.
Results may differ from the reference program's by a relative error of at most 0.003.
Values may be sent and summed in bfloat16 or wider, within the bound.
A program may use at most 64 MiB of HBM per device.

```python
import math
import jax
import jax.numpy as jnp
import numpy as np
from jax import lax

F = 16384
K = 512
T_DEV = 256
SEGS = 64
NR = 32
LAG_MAX = 64
FRAMES = 2048
REPS = 2
SEG_MOST = 256
N_FEAT = 2


def draw_frames(key, part):
    span = 2 * LAG_MAX

    def one_run(run_key):
        slow_part = jnp.clip(jax.random.normal(jax.random.fold_in(run_key, 1), (FRAMES // span + 2, F), jnp.float32), -5.0, 5.0)
        slow_full = jnp.repeat(slow_part, span, axis=0)[LAG_MAX:LAG_MAX + FRAMES]
        fast_part = jnp.clip(jax.random.normal(jax.random.fold_in(run_key, 2), (FRAMES, F), jnp.float32), -5.0, 5.0)
        ramp = jnp.exp(jnp.log(3.0) * jnp.arange(FRAMES, dtype=jnp.float32) / FRAMES)
        values = (slow_full + 0.6 * fast_part) * ramp[:, None]
        return values.astype(jnp.bfloat16)
    run_keys = jax.random.split(jax.random.fold_in(key, 7), REPS)
    return lax.map(one_run, run_keys)


def draw_lags(key, part):
    chosen = jax.random.randint(jax.random.fold_in(key, 21), (), 0, REPS)
    others = jax.random.randint(jax.random.fold_in(key, 22), (REPS,), 1, LAG_MAX + 1)
    return jnp.where(jnp.arange(REPS) == chosen, LAG_MAX, others).astype(jnp.int32)


def block_levels(key, extent, cuts, smallest, high):
    def one(position, blocks):
        steps = jax.random.uniform(jax.random.fold_in(jax.random.fold_in(key, 6), position), (blocks,), jnp.float32, smallest / len(cuts), high / len(cuts))
        return jnp.repeat(jnp.exp(steps), extent[position] // blocks).reshape((-1,) + (1,) * (len(extent) - position - 1))

    gain = one(*cuts[0])
    for cut in cuts[1:]:
        gain = gain * one(*cut)
    return gain


def length_profile(amount, total, bound, slope):
    weights = [(1 << 20) // math.isqrt(grade ** slope) + 1 for grade in range(2, amount + 1)]
    spare, counts = total - bound - (amount - 1), [1] * (amount - 1)
    while spare > 0:
        movable = [i for i in range(amount - 1) if counts[i] < bound]
        whole, remaining = sum([weights[i] for i in movable]), spare
        for i in movable:
            extra = min(bound - counts[i], max(1, remaining * weights[i] // whole), spare)
            counts[i] = counts[i] + extra
            spare = spare - extra
    return np.array([bound] + counts)


def uneven_parts(own_key, number_of, total, reach, lean):
    if number_of == 2:
        one = jax.random.randint(own_key, (), max(1, total - reach), min(reach, total - 1) + 1)
        return jnp.stack([one, total - one])
    lengths = jnp.asarray(length_profile(number_of, total, reach, lean), jnp.int32)
    couples = (number_of - 1) // 2
    donor, taker = lengths[1:1 + 2 * couples:2], lengths[2:2 + 2 * couples:2]
    room = jnp.minimum(donor - 1, reach - taker)
    passed = jax.random.randint(jax.random.fold_in(own_key, 1), (couples,), 0, 1 << 20) % (room + 1)
    lengths = lengths.at[1:1 + 2 * couples:2].set(donor - passed).at[2:2 + 2 * couples:2].set(taker + passed)
    return lengths[jax.random.permutation(jax.random.fold_in(own_key, 2), number_of)]


def gaussian(rng, shape, scale, bound, shards=(), kind=jnp.bfloat16):
    loudness = block_levels(rng, shape, shards, -0.22, 0.18) if shards else 1.0
    values = jax.random.normal(rng, shape, jnp.float32) * scale * loudness
    return jnp.minimum(jnp.maximum(values, -bound), bound).astype(kind)


def setup_inputs(seed: int = 0) -> dict:
    arg_keys = jax.random.split(jax.random.key(seed), 7)
    return {
        "frames": draw_frames(jax.random.fold_in(arg_keys[6], 71), 0),
        "panel_low": gaussian(arg_keys[1], (F, K), F ** -0.5, 0.046875, ((0, 2), (1, 8))),
        "panel_high": gaussian(arg_keys[2], (F, K), F ** -0.5, 0.046875, ((0, 2), (1, 8))),
        "lags": draw_lags(jax.random.fold_in(arg_keys[6], 71), 0),
        "seg_lengths": jax.vmap(lambda own: uneven_parts(own, SEGS, FRAMES, SEG_MOST, 2))(jax.random.split(arg_keys[4], REPS)).reshape((REPS, SEGS)).astype(jnp.int32),
        "ridge": jnp.clip(jnp.exp(jax.random.uniform(arg_keys[5], (NR,), jnp.float32, math.log(0.01), math.log(10.0))), 0.01, 10.0),
    }


def project_block(frame_block, panels):
    width = F // N_FEAT
    summed = jnp.zeros((frame_block.shape[0], 2 * K), jnp.float32)
    for feature_group in range(N_FEAT):
        partial_term = jnp.dot(frame_block[:, feature_group * width:(feature_group + 1) * width],
                               panels[feature_group * width:(feature_group + 1) * width],
                               preferred_element_type=jnp.float32)
        rounded = lax.optimization_barrier(partial_term.astype(jnp.bfloat16))
        summed = summed + rounded.astype(jnp.float32)
    return summed.astype(jnp.bfloat16)


def reference(frames, panel_low, panel_high, lags, seg_lengths, ridge):
    panels = jnp.concatenate([panel_low, panel_high], axis=1)
    frame_blocks = frames.reshape(REPS * FRAMES // T_DEV, T_DEV, F)
    basis = lax.map(lambda blk_rows: project_block(blk_rows, panels), frame_blocks)
    basis = basis.reshape(REPS, FRAMES, 2 * K)
    positions = jnp.arange(FRAMES, dtype=jnp.int32)
    cov_inst = jnp.zeros((2 * K, 2 * K), jnp.float32)
    cov_cross = jnp.zeros((2 * K, 2 * K), jnp.float32)
    cov_lagged = jnp.zeros((2 * K, 2 * K), jnp.float32)
    for replica in range(REPS):
        lag_now = lags[replica].astype(jnp.int32)
        padded = jnp.concatenate([basis[replica], jnp.zeros((LAG_MAX, 2 * K), jnp.bfloat16)], axis=0)
        lagged = lax.dynamic_slice_in_dim(padded, lag_now, FRAMES, 0)
        seg_ends = jnp.cumsum(seg_lengths[replica]).astype(jnp.int32)
        end_of = jnp.min(jnp.where(seg_ends[None, :] > positions[:, None], seg_ends[None, :], FRAMES), axis=1)
        keep_mask = (positions + lag_now < end_of).astype(jnp.bfloat16)[:, None]
        masked = basis[replica] * keep_mask
        lag_masked = lagged * keep_mask
        cov_inst = cov_inst + jnp.dot(masked.T, basis[replica], preferred_element_type=jnp.float32)
        cov_cross = cov_cross + jnp.dot(masked.T, lagged, preferred_element_type=jnp.float32)
        cov_lagged = cov_lagged + jnp.dot(lag_masked.T, lagged, preferred_element_type=jnp.float32)
    inverse_count = 1.0 / (REPS * FRAMES)
    cov_inst = cov_inst * inverse_count
    cov_cross = cov_cross * inverse_count
    cov_lagged = cov_lagged * inverse_count
    diag_inst = jnp.diagonal(cov_inst)
    diag_lagged = jnp.diagonal(cov_lagged)
    inverse_lagged = 1.0 / (diag_lagged[:, None] + ridge[None, :])
    weighted = jnp.dot(jnp.square(cov_cross), inverse_lagged, precision=lax.Precision.HIGHEST,
                       preferred_element_type=jnp.float32)
    scores = weighted / (diag_inst[:, None] + ridge[None, :])
    covariances = jnp.stack([cov_inst, cov_cross, cov_lagged], axis=0)
    return (covariances, scores)
```

```python
import functools
import jax
import jax.numpy as jnp
from jax import lax
from jax.experimental import pallas as pl
from jax.experimental.pallas import tpu as pltpu
from jax.sharding import PartitionSpec as P

MESH = pl.DeviceIdType.MESH
N_CHUNK = 4
TILE = 1024


def passed_along(shard, axis, by):
    length = lax.axis_size(axis)
    pairs = [(i, i + by) for i in range(length) if 0 <= i + by < length]
    return lax.ppermute(shard, axis, pairs)


def local_general(frames, panel_low, panel_high, lags, seg_lengths, ridge):
    local_frames = frames[0]
    t_local = local_frames.shape[0]
    lag_most = t_local // 4
    n_time = lax.axis_size("tm")
    n_feature = lax.axis_size("feat")
    n_replica = lax.axis_size("rep")
    panel_cols = panel_low.shape[1] * n_time
    basis_width = 2 * panel_cols
    per_device = basis_width // (n_time * n_feature * n_replica)
    time_index = lax.axis_index("tm")
    feature_index = lax.axis_index("feat")
    replica_index = lax.axis_index("rep")
    stacked = jnp.stack([panel_low, panel_high], axis=0)
    partial_sum = jnp.einsum(
        "tf,pfk->tpk",
        local_frames,
        lax.all_gather(stacked, "tm", axis=2, tiled=True),
        preferred_element_type=jnp.float32,
    )
    partial_sum = partial_sum.reshape(local_frames.shape[0], basis_width)
    partial_rounded = partial_sum.astype(jnp.bfloat16)
    summed = lax.psum(partial_rounded, "feat").astype(jnp.float32).astype(jnp.bfloat16)
    next_basis = passed_along(summed[:lag_most], "tm", -1)
    extended = jnp.concatenate([summed, next_basis], axis=0)
    lag_now = lags[0]
    lagged = lax.dynamic_slice_in_dim(extended, lag_now, t_local, 0)
    frame_total = t_local * n_time
    positions = time_index * t_local + jnp.arange(t_local, dtype=jnp.int32)
    seg_ends = jnp.cumsum(seg_lengths[0])
    end_of = jnp.min(
        jnp.where(seg_ends[None, :] > positions[:, None], seg_ends[None, :], frame_total), axis=1
    )
    keep_mask = (positions + lag_now < end_of).astype(jnp.bfloat16)[:, None]
    masked = summed * keep_mask
    lag_masked = lagged * keep_mask

    def own_group(values):
        shaped = values.reshape(t_local, n_time, n_feature, n_replica * per_device)
        return lax.dynamic_index_in_dim(shaped, feature_index, 2, keepdims=False).reshape(
            t_local, -1
        )

    group_masked = own_group(masked)
    group_lagged = own_group(lag_masked)
    term_inst = jnp.einsum("ti,tj->ij", group_masked, summed, preferred_element_type=jnp.float32)
    term_cross = jnp.einsum("ti,tj->ij", group_masked, lagged, preferred_element_type=jnp.float32)
    term_lagged = jnp.einsum("ti,tj->ij", group_lagged, lagged, preferred_element_type=jnp.float32)
    row_block = lax.psum_scatter(
        jnp.stack([term_inst, term_cross, term_lagged], axis=1),
        ("tm", "rep"),
        scatter_dimension=0,
        tiled=True,
    )
    inverse_count = 1.0 / (frame_total * n_replica)
    cov_rows = jnp.transpose(row_block, (1, 0, 2)) * inverse_count
    local_var = jnp.sum(jnp.square(lag_masked.astype(jnp.float32)), axis=0)
    diag_lagged = lax.psum(local_var, ("tm", "rep")) * inverse_count
    return finish(cov_rows, diag_lagged, ridge)


def finish(cov_rows, diag_lagged, ridge):
    per_device, basis_width = cov_rows.shape[1:]
    device_linear = (
        lax.axis_index("tm") * lax.axis_size("feat") + lax.axis_index("feat")
    ) * lax.axis_size("rep") + lax.axis_index("rep")
    own_index = device_linear * per_device + jnp.arange(per_device, dtype=jnp.int32)
    selector = (jnp.arange(basis_width, dtype=jnp.int32)[None, :] == own_index[:, None]).astype(
        jnp.float32
    )
    diag_inst = jnp.sum(cov_rows[0] * selector, axis=1)
    inverse_lagged = 1.0 / (diag_lagged[:, None] + ridge[None, :])
    weighted = jnp.dot(
        jnp.square(cov_rows[1]),
        inverse_lagged,
        precision=lax.Precision.HIGHEST,
        preferred_element_type=jnp.float32,
    )
    scores = weighted / (diag_inst[:, None] + ridge[None, :])
    return (cov_rows, scores)


def line_gather(n_z, z, chunks, own_src, slot, send_up, send_down, ready, sems):
    up_sem, down_sem, recv_sem = sems

    def copy(src, place, k, sem, target):
        return pltpu.make_async_remote_copy(
            src_ref=src, dst_ref=slot(place, k), send_sem=sem.at[place, k],
            recv_sem=recv_sem.at[place, k], device_id=target, device_id_type=MESH)

    for k in chunks:
        @pl.when(z + 1 < n_z)
        def _():
            copy(own_src(k), z, k, up_sem, send_up).start()

        @pl.when(z > 0)
        def _():
            copy(own_src(k), z, k, down_sem, send_down).start()

        ready(z, k, True)
    for step in range(1, n_z):
        for k in chunks:
            @pl.when(z - step >= 0)
            def _():
                place = z - step
                copy(slot(place, k), place, k, up_sem, send_up).wait_recv()

                @pl.when(z + 1 < n_z)
                def _():
                    copy(slot(place, k), place, k, up_sem, send_up).start()

                ready(place, k, False)

            @pl.when(z + step < n_z)
            def _():
                place = z + step
                copy(slot(place, k), place, k, down_sem, send_down).wait_recv()

                @pl.when(z > 0)
                def _():
                    copy(slot(place, k), place, k, down_sem, send_down).start()

                ready(place, k, False)

    def finish_sends():
        for place in range(n_z):
            for k in chunks:
                @pl.when(jnp.logical_and(z + 1 < n_z, place <= z))
                def _():
                    copy(slot(place, k), place, k, up_sem, send_up).wait_send()

                @pl.when(jnp.logical_and(z > 0, place >= z))
                def _():
                    copy(slot(place, k), place, k, down_sem, send_down).wait_send()

    return finish_sends


def kernel(n_time, frames_ref, panel_ref, out_ref, all_frames, all_panels, total, part, other, summed,
           local_sem, f_send, f_recv, p_up, p_down, p_recv, px_send, px_recv,
           c_sem, y_sem, b_up, b_down, b_recv, bx_send, bx_recv, bc_send, bc_recv):
    n_z = n_time // 2
    tm, core, run = lax.axis_index("tm"), lax.axis_index("feat"), lax.axis_index("rep")
    z, x = tm // 2, tm % 2
    to_up = (jnp.minimum(tm + 2, n_time - 2 + x), core, run)
    to_down = (jnp.maximum(tm - 2, x), core, run)
    to_x = (z * 2 + (1 - x), core, run)
    to_y = (tm, core, 1 - run)
    to_core = (tm, 1 - core, run)
    n_features = frames_ref.shape[1]
    cut = n_features // N_CHUNK
    chunks = range(N_CHUNK)

    own_panel = pltpu.make_async_copy(panel_ref, all_panels.at[tm], local_sem.at[0])
    own_panel.start()
    own_frames = pltpu.make_async_copy(frames_ref, all_frames.at[run], local_sem.at[1])
    own_frames.start()

    barrier = pltpu.get_barrier_semaphore()

    @pl.when(z + 1 < n_z)
    def _():
        pl.semaphore_signal(barrier, inc=1, device_id=to_up, device_id_type=MESH)

    @pl.when(z > 0)
    def _():
        pl.semaphore_signal(barrier, inc=1, device_id=to_down, device_id_type=MESH)

    for target in (to_x, to_y, to_core):
        pl.semaphore_signal(barrier, inc=1, device_id=target, device_id_type=MESH)

    @pl.when(jnp.logical_or(z == 0, z == n_z - 1))
    def _():
        pl.semaphore_wait(barrier, 4)

    @pl.when(jnp.logical_and(z > 0, z < n_z - 1))
    def _():
        pl.semaphore_wait(barrier, 5)

    def lanes(k):
        return pl.ds(k * cut, cut)

    def frame_copy(k):
        return pltpu.make_async_remote_copy(
            src_ref=frames_ref.at[:, lanes(k)], dst_ref=all_frames.at[run, :, lanes(k)],
            send_sem=f_send.at[k], recv_sem=f_recv.at[k], device_id=to_y, device_id_type=MESH)

    for k in chunks:
        frame_copy(k).start()

    def panel_slot(place, k):
        return all_panels.at[place * 2 + x, :, lanes(k)]

    def panel_x(src, place, k):
        return pltpu.make_async_remote_copy(
            src_ref=src, dst_ref=panel_slot(place, k), send_sem=px_send.at[place, k],
            recv_sem=px_recv.at[place, k], device_id=to_x, device_id_type=MESH)

    def panel_ready(place, k, own):
        panel_x(panel_ref.at[:, lanes(k)] if own else panel_slot(place, k), place, k).start()

    panel_sends = line_gather(
        n_z, z, chunks, lambda k: panel_ref.at[:, lanes(k)], panel_slot, to_up, to_down,
        panel_ready, (p_up, p_down, p_recv))
    total[...] = jnp.zeros_like(total)
    own_panel.wait()
    own_frames.wait()
    for k in chunks:
        for place in range(n_z):
            pltpu.make_async_remote_copy(
                src_ref=panel_slot(place, k), dst_ref=all_panels.at[place * 2 + (1 - x), :, lanes(k)],
                send_sem=px_send.at[place, k], recv_sem=px_recv.at[place, k],
                device_id=to_x, device_id_type=MESH).wait_recv()
        pltpu.make_async_remote_copy(
            src_ref=frames_ref.at[:, lanes(k)], dst_ref=all_frames.at[1 - run, :, lanes(k)],
            send_sem=f_send.at[k], recv_sem=f_recv.at[k], device_id=to_y,
            device_id_type=MESH).wait_recv()

        @pl.loop(0, cut // TILE)
        def _(i):
            at = pl.ds(pl.multiple_of(k * cut + i * TILE, TILE), TILE)
            left = all_frames[:, :, at].reshape(total.shape[0], TILE)
            right = all_panels[:, :, at].reshape(total.shape[1], TILE)
            total[...] += lax.dot_general(
                left, right, (((1,), (1,)), ((), ())), preferred_element_type=jnp.float32)

    half = part.shape[2]
    part[...] = total[...].astype(jnp.bfloat16).reshape(part.shape)
    core_copy = pltpu.make_async_remote_copy(
        src_ref=part.at[:, 1 - core], dst_ref=other, send_sem=c_sem.at[0], recv_sem=c_sem.at[1],
        device_id=to_core, device_id_type=MESH)
    core_copy.start()
    core_copy.wait_recv()
    both = part[:, core].astype(jnp.float32) + other[...].astype(jnp.float32)
    summed[...] = both.astype(jnp.bfloat16)
    y_copy = pltpu.make_async_remote_copy(
        src_ref=summed.at[1 - run], dst_ref=out_ref.at[run, tm, core], send_sem=y_sem.at[0],
        recv_sem=y_sem.at[1], device_id=to_y, device_id_type=MESH)
    y_copy.start()
    out_ref[run, tm, core] = summed[run]

    def side(k):
        return run if k == 0 else 1 - run

    def basis_x(place, k):
        ref = out_ref.at[side(k), place * 2 + x, core]
        return pltpu.make_async_remote_copy(
            src_ref=ref, dst_ref=ref, send_sem=bx_send.at[place, k],
            recv_sem=bx_recv.at[place, k], device_id=to_x, device_id_type=MESH)

    def basis_core(place, k, from_x):
        at = place * 2 + (1 - x if from_x else x)
        ref = out_ref.at[side(k), at, core]
        return pltpu.make_async_remote_copy(
            src_ref=ref, dst_ref=ref, send_sem=bc_send.at[at, k],
            recv_sem=bc_recv.at[at, k], device_id=to_core, device_id_type=MESH)

    def basis_slot(place, k):
        return out_ref.at[side(k), place * 2 + x, core]

    def basis_own(k):
        if k == 1:
            pltpu.make_async_remote_copy(
                src_ref=summed.at[1 - run], dst_ref=out_ref.at[1 - run, tm, core],
                send_sem=y_sem.at[0], recv_sem=y_sem.at[1], device_id=to_y,
                device_id_type=MESH).wait_recv()
        return basis_slot(z, k)

    own_refs = {}

    def basis_ready(place, k, own):
        basis_x(place, k).start()
        basis_core(place, k, False).start()

    def basis_src(k):
        return basis_slot(z, k)

    def gather(k_list, first):
        return line_gather(n_z, z, k_list, basis_src, basis_slot, to_up, to_down, basis_ready,
                           (b_up, b_down, b_recv))

    basis_own(1)
    basis_sends = gather(range(2), True)
    for place in range(n_z):
        for k in range(2):
            pltpu.make_async_remote_copy(
                src_ref=basis_slot(place, k), dst_ref=out_ref.at[side(k), place * 2 + (1 - x), core],
                send_sem=bx_send.at[place, k], recv_sem=bx_recv.at[place, k],
                device_id=to_x, device_id_type=MESH).wait_recv()
            basis_core(place, k, True).start()
    for k in range(2):
        for at in range(n_time):
            theirs = out_ref.at[side(k), at, 1 - core]
            pltpu.make_async_remote_copy(
                src_ref=theirs, dst_ref=theirs, send_sem=bc_send.at[at, k],
                recv_sem=bc_recv.at[at, k], device_id=to_core, device_id_type=MESH).wait_recv()
    for k in chunks:
        frame_copy(k).wait_send()
        for place in range(n_z):
            panel_x(panel_slot(place, k), place, k).wait_send()
    panel_sends()
    basis_sends()
    core_copy.wait_send()
    y_copy.wait_send()
    for k in range(2):
        for place in range(n_z):
            basis_x(place, k).wait_send()
            basis_core(place, k, False).wait_send()
            basis_core(place, k, True).wait_send()


def gathered_basis(frames, panel, n_time):
    t_local, features = frames.shape
    width = panel.shape[0] * n_time
    n_z = n_time // 2
    half = t_local // 2
    dma = pltpu.SemaphoreType.DMA
    vmem = pltpu.VMEM
    line = [dma((n_z, N_CHUNK))] * 5
    basis_line = [dma((n_z, 2))] * 5
    flops = 2 * 2 * t_local * features * width
    return pl.pallas_call(
        functools.partial(kernel, n_time),
        out_shape=jax.ShapeDtypeStruct((2, n_time, 2, half, width), jnp.bfloat16),
        in_specs=[pl.BlockSpec(memory_space=pl.ANY)] * 2,
        out_specs=pl.BlockSpec(memory_space=pltpu.VMEM),
        scratch_shapes=[
            vmem((2, t_local, features), jnp.bfloat16),
            vmem((n_time, panel.shape[0], features), jnp.bfloat16),
            vmem((2 * t_local, width), jnp.float32),
            vmem((2, 2, half, width), jnp.bfloat16),
            vmem((2, half, width), jnp.bfloat16),
            vmem((2, half, width), jnp.bfloat16),
            dma((2,)), dma((N_CHUNK,)), dma((N_CHUNK,)),
            *line, dma((2,)), dma((2,)), *basis_line,
            dma((n_time, 2)), dma((n_time, 2)),
        ],
        compiler_params=pltpu.CompilerParams(
            collective_id=0, has_side_effects=True, vmem_limit_bytes=56 * 2**20),
        cost_estimate=pl.CostEstimate(flops=flops, bytes_accessed=16 * 2**20, transcendentals=0),
    )(frames, panel)


def local(frames, panel_low, panel_high, lags, seg_lengths, ridge):
    t_local = frames.shape[1]
    n_time = lax.axis_size("tm")
    tm, core, run = lax.axis_index("tm"), lax.axis_index("feat"), lax.axis_index("rep")
    panel = jnp.where(run == 0, panel_low.T, panel_high.T)
    basis = gathered_basis(frames[0], panel, n_time)
    width = basis.shape[-1]
    total = t_local * n_time
    basis = basis.reshape(2, total, width)
    rows = 2 * width // (n_time * 2)
    lag_most = t_local // 4
    lag_now = lags[0]
    positions = jnp.arange(total, dtype=jnp.int32)
    seg_ends = jnp.cumsum(seg_lengths[0])
    end_of = jnp.min(
        jnp.where(seg_ends[None, :] > positions[:, None], seg_ends[None, :], total), axis=1
    )
    keep = (positions + lag_now < end_of).astype(jnp.bfloat16)

    def later(values):
        spare = jnp.zeros((lag_most,) + values.shape[1:], values.dtype)
        return lax.dynamic_slice_in_dim(
            jnp.concatenate([spare, values], axis=0), lag_most - lag_now, total, 0)

    later_keep = later(keep)
    first = (tm * 2 + core) * rows
    own = lax.dynamic_slice(basis, (first // width, 0, first % width), (1, total, rows))[0]
    masked = own * keep[:, None]
    left = jnp.concatenate([masked, later(masked), own * later_keep[:, None]], axis=1)
    terms = jnp.einsum("ta,htj->ahj", left, basis, preferred_element_type=jnp.float32)
    terms = terms.reshape(3, 2, rows // 2, 2 * width)
    variance = jnp.sum(
        jnp.square(basis.astype(jnp.float32)) * later_keep.astype(jnp.float32)[None, :, None], axis=1
    ).reshape(1, 2 * width)
    theirs = lax.dynamic_index_in_dim(terms, 1 - run, 1, keepdims=False).reshape(-1, 2 * width)
    mine = lax.dynamic_index_in_dim(terms, run, 1, keepdims=False)
    received = lax.ppermute(
        jnp.concatenate([theirs, variance], axis=0), "rep", [(0, 1), (1, 0)])
    inverse_count = 1.0 / (total * 2)
    cov_rows = (mine + received[:-1].reshape(mine.shape)) * inverse_count
    diag_lagged = (variance[0] + received[-1]) * inverse_count
    return finish(cov_rows, diag_lagged, ridge)


def solution(mesh):
    in_specs = (
        P("rep", "tm", "feat"),
        P("feat", "tm"),
        P("feat", "tm"),
        P("rep"),
        P("rep", None),
        P(),
    )
    out_specs = (P(None, ("tm", "feat", "rep"), None), P(("tm", "feat", "rep"), None))
    shape = dict(mesh.shape)
    paired = shape["feat"] == 2 and shape["rep"] == 2 and shape["tm"] == 8
    body = local if paired else local_general
    return jax.shard_map(body, mesh=mesh, in_specs=in_specs, out_specs=out_specs, check_vma=False)
```

```python
import functools
import jax
import jax.numpy as jnp
from jax import lax
from jax.experimental import pallas as pl
from jax.experimental.pallas import tpu as pltpu
from jax.sharding import PartitionSpec as P

MESH = pl.DeviceIdType.MESH
TILE = 1024


def passed_along(shard, axis, by):
    length = lax.axis_size(axis)
    pairs = [(i, i + by) for i in range(length) if 0 <= i + by < length]
    return lax.ppermute(shard, axis, pairs)


def local_general(frames, panel_low, panel_high, lags, seg_lengths, ridge):
    local_frames = frames[0]
    t_local = local_frames.shape[0]
    lag_most = t_local // 4
    n_time = lax.axis_size("tm")
    n_feature = lax.axis_size("feat")
    n_replica = lax.axis_size("rep")
    panel_cols = panel_low.shape[1] * n_time
    basis_width = 2 * panel_cols
    per_device = basis_width // (n_time * n_feature * n_replica)
    time_index = lax.axis_index("tm")
    feature_index = lax.axis_index("feat")
    replica_index = lax.axis_index("rep")
    stacked = jnp.stack([panel_low, panel_high], axis=0)
    partial_sum = jnp.einsum(
        "tf,pfk->tpk",
        local_frames,
        lax.all_gather(stacked, "tm", axis=2, tiled=True),
        preferred_element_type=jnp.float32,
    )
    partial_sum = partial_sum.reshape(local_frames.shape[0], basis_width)
    partial_rounded = partial_sum.astype(jnp.bfloat16)
    summed = lax.psum(partial_rounded, "feat").astype(jnp.float32).astype(jnp.bfloat16)
    next_basis = passed_along(summed[:lag_most], "tm", -1)
    extended = jnp.concatenate([summed, next_basis], axis=0)
    lag_now = lags[0]
    lagged = lax.dynamic_slice_in_dim(extended, lag_now, t_local, 0)
    frame_total = t_local * n_time
    positions = time_index * t_local + jnp.arange(t_local, dtype=jnp.int32)
    seg_ends = jnp.cumsum(seg_lengths[0])
    end_of = jnp.min(
        jnp.where(seg_ends[None, :] > positions[:, None], seg_ends[None, :], frame_total), axis=1
    )
    keep_mask = (positions + lag_now < end_of).astype(jnp.bfloat16)[:, None]
    masked = summed * keep_mask
    lag_masked = lagged * keep_mask

    def own_group(values):
        shaped = values.reshape(t_local, n_time, n_feature, n_replica * per_device)
        return lax.dynamic_index_in_dim(shaped, feature_index, 2, keepdims=False).reshape(
            t_local, -1
        )

    group_masked = own_group(masked)
    group_lagged = own_group(lag_masked)
    term_inst = jnp.einsum("ti,tj->ij", group_masked, summed, preferred_element_type=jnp.float32)
    term_cross = jnp.einsum("ti,tj->ij", group_masked, lagged, preferred_element_type=jnp.float32)
    term_lagged = jnp.einsum("ti,tj->ij", group_lagged, lagged, preferred_element_type=jnp.float32)
    row_block = lax.psum_scatter(
        jnp.stack([term_inst, term_cross, term_lagged], axis=1),
        ("tm", "rep"),
        scatter_dimension=0,
        tiled=True,
    )
    inverse_count = 1.0 / (frame_total * n_replica)
    cov_rows = jnp.transpose(row_block, (1, 0, 2)) * inverse_count
    local_var = jnp.sum(jnp.square(lag_masked.astype(jnp.float32)), axis=0)
    diag_lagged = lax.psum(local_var, ("tm", "rep")) * inverse_count
    return finish(cov_rows, diag_lagged, ridge)


def finish(cov_rows, diag_lagged, ridge):
    per_device, basis_width = cov_rows.shape[1:]
    device_linear = (
        lax.axis_index("tm") * lax.axis_size("feat") + lax.axis_index("feat")
    ) * lax.axis_size("rep") + lax.axis_index("rep")
    own_index = device_linear * per_device + jnp.arange(per_device, dtype=jnp.int32)
    selector = (jnp.arange(basis_width, dtype=jnp.int32)[None, :] == own_index[:, None]).astype(
        jnp.float32
    )
    diag_inst = jnp.sum(cov_rows[0] * selector, axis=1)
    inverse_lagged = 1.0 / (diag_lagged[:, None] + ridge[None, :])
    weighted = jnp.dot(
        jnp.square(cov_rows[1]),
        inverse_lagged,
        precision=lax.Precision.HIGHEST,
        preferred_element_type=jnp.float32,
    )
    scores = weighted / (diag_inst[:, None] + ridge[None, :])
    return (cov_rows, scores)


def line_gather(n_z, z, chunks, slot, send_up, send_down, begin, ready, after_first, sems):
    up_sem, down_sem, recv_sem = sems

    def copy(place, k, sem, target):
        return pltpu.make_async_remote_copy(
            src_ref=slot(place, k), dst_ref=slot(place, k), send_sem=sem.at[place, k],
            recv_sem=recv_sem.at[place, k], device_id=target, device_id_type=MESH)

    for k in chunks:
        begin(k)

        @pl.when(z + 1 < n_z)
        def _():
            copy(z, k, up_sem, send_up).start()

        @pl.when(z > 0)
        def _():
            copy(z, k, down_sem, send_down).start()

        ready(z, k)
    for step in range(1, n_z):
        for k in chunks:
            @pl.when(z - step >= 0)
            def _():
                place = z - step
                copy(place, k, up_sem, send_up).wait_recv()

                @pl.when(z + 1 < n_z)
                def _():
                    copy(place, k, up_sem, send_up).start()

                ready(place, k)

            @pl.when(z + step < n_z)
            def _():
                place = z + step
                copy(place, k, down_sem, send_down).wait_recv()

                @pl.when(z > 0)
                def _():
                    copy(place, k, down_sem, send_down).start()

                ready(place, k)

        if step == 1:
            after_first()

    def finish_sends():
        for place in range(n_z):
            for k in chunks:
                @pl.when(jnp.logical_and(z + 1 < n_z, place <= z))
                def _():
                    copy(place, k, up_sem, send_up).wait_send()

                @pl.when(jnp.logical_and(z > 0, place >= z))
                def _():
                    copy(place, k, down_sem, send_down).wait_send()

    return finish_sends


def kernel(n_time, frames_ref, low_ref, high_ref, out_ref, all_frames, all_panels, total, part, other,
           y_out, y_in, local_sem, f_send, f_recv, p_up, p_down, p_recv, px_send, px_recv,
           pz_send, pz_recv, c_send, c_recv, y_send, y_recv,
           b_up, b_down, b_recv, bx_send, bx_recv, bc_send, bc_recv):
    n_z = n_time // 2
    tm, core, run = lax.axis_index("tm"), lax.axis_index("feat"), lax.axis_index("rep")
    z, x = tm // 2, tm % 2
    pair = z + 1 - 2 * (z % 2)
    to_up = (jnp.minimum(tm + 2, n_time - 2 + x), core, run)
    to_down = (jnp.maximum(tm - 2, x), core, run)
    to_pair = (pair * 2 + x, core, run)
    to_x = (z * 2 + (1 - x), core, run)
    to_y = (tm, core, 1 - run)
    to_core = (tm, 1 - core, run)
    features = all_frames.shape[2]
    cut = features // 2
    chunks = range(4)
    by_pair = (2, 3)

    own_lanes = pl.ds(pl.multiple_of(run * features, features), features)
    their_lanes = pl.ds(pl.multiple_of((1 - run) * features, features), features)
    own_low = pltpu.make_async_copy(low_ref.at[:, own_lanes], all_panels.at[0, tm], local_sem.at[0])
    own_high = pltpu.make_async_copy(high_ref.at[:, own_lanes], all_panels.at[1, tm], local_sem.at[1])
    own_frames = pltpu.make_async_copy(
        frames_ref.at[:, own_lanes], all_frames.at[run], local_sem.at[2])
    own_low.start()
    own_high.start()
    own_frames.start()

    barrier = pltpu.get_barrier_semaphore()

    @pl.when(z + 1 < n_z)
    def _():
        pl.semaphore_signal(barrier, inc=1, device_id=to_up, device_id_type=MESH)

    @pl.when(z > 0)
    def _():
        pl.semaphore_signal(barrier, inc=1, device_id=to_down, device_id_type=MESH)

    for target in (to_x, to_y, to_core):
        pl.semaphore_signal(barrier, inc=1, device_id=target, device_id_type=MESH)

    @pl.when(jnp.logical_or(z == 0, z == n_z - 1))
    def _():
        pl.semaphore_wait(barrier, 4)

    @pl.when(jnp.logical_and(z > 0, z < n_z - 1))
    def _():
        pl.semaphore_wait(barrier, 5)

    def frame_copy(slot_run):
        return pltpu.make_async_remote_copy(
            src_ref=frames_ref.at[:, their_lanes], dst_ref=all_frames.at[slot_run],
            send_sem=f_send.at[0], recv_sem=f_recv.at[0], device_id=to_y, device_id_type=MESH)

    def panel_ref(place, side, k):
        return all_panels.at[k // 2, place * 2 + side, :, pl.ds((k % 2) * cut, cut)]

    def panel_slot(place, k):
        return panel_ref(place, x, k)

    def panel_x(place, side, k):
        ref = panel_ref(place, side, k)
        return pltpu.make_async_remote_copy(
            src_ref=ref, dst_ref=ref, send_sem=px_send.at[place, k],
            recv_sem=px_recv.at[place, k], device_id=to_x, device_id_type=MESH)

    def panel_pair(place, k):
        ref = panel_ref(place, 1 - x, k)
        return pltpu.make_async_remote_copy(
            src_ref=ref, dst_ref=ref, send_sem=pz_send.at[k], recv_sem=pz_recv.at[k],
            device_id=to_pair, device_id_type=MESH)

    def unless_by_pair(place, k, act):
        if k in by_pair:
            pl.when(place != pair)(act)
        else:
            act()

    def panel_begin(k):
        if k == 0:
            own_low.wait()
        if k == 2:
            own_high.wait()

    def panel_ready(place, k):
        unless_by_pair(place, k, lambda: panel_x(place, x, k).start())

    def pass_to_pair():
        for k in by_pair:
            panel_x(z, 1 - x, k).wait_recv()
            panel_pair(z, k).start()

    frame_copy(run).start()
    panel_sends = line_gather(
        n_z, z, chunks, panel_slot, to_up, to_down, panel_begin, panel_ready, pass_to_pair,
        (p_up, p_down, p_recv))
    own_frames.wait()
    frame_copy(1 - run).wait_recv()
    far = z // 2
    rows, columns = total.shape
    block = all_panels.shape[2] * 2
    for turn, place in enumerate((z, pair, 2 - far, 3 - 3 * far)):
        for k in chunks:
            if turn == 0 and k in by_pair:
                continue
            if turn == 1 and k in by_pair:
                panel_pair(place, k).wait_recv()
            else:
                panel_x(place, 1 - x, k).wait_recv()

        def term(i, so_far):
            at = pl.ds(pl.multiple_of(i * TILE, TILE), TILE)
            left = all_frames[:, :, at].reshape(rows, TILE)
            right = all_panels[:, pl.ds(place * 2, 2), :, at].reshape(2 * block, TILE)
            return so_far + lax.dot_general(
                left, right, (((1,), (1,)), ((), ())), preferred_element_type=jnp.float32)

        result = lax.fori_loop(
            0, features // TILE, term, jnp.zeros((rows, 2 * block), jnp.float32))
        for panel in range(2):
            at = pl.ds(pl.multiple_of(panel * (columns // 2) + place * block, block), block)
            total[:, at] = result[:, panel * block:(panel + 1) * block]
            part[:, :, :, at] = result[:, panel * block:(panel + 1) * block].astype(
                jnp.bfloat16).reshape(2, 2, rows // 4, block)

    half = rows // 4
    wide = columns // 2
    own_rows = pl.multiple_of(core * half, half)

    def across(h):
        return pl.ds(h * wide, wide)

    def core_copy(h):
        return pltpu.make_async_remote_copy(
            src_ref=part.at[:, 1 - core, :, across(h)], dst_ref=other.at[:, :, across(h)],
            send_sem=c_send.at[h], recv_sem=c_recv.at[h], device_id=to_core, device_id_type=MESH)

    def y_copy(h):
        return pltpu.make_async_remote_copy(
            src_ref=y_out.at[:, across(h)], dst_ref=y_in.at[:, across(h)],
            send_sem=y_send.at[h], recv_sem=y_recv.at[h], device_id=to_y, device_id_type=MESH)

    def both_cores(which, h):
        first = pl.multiple_of(which * 2 * half + own_rows, half)
        return total[pl.ds(first, half), across(h)] + other[which, :, across(h)].astype(jnp.float32)

    for h in range(2):
        core_copy(h).start()
    for h in range(2):
        core_copy(h).wait_recv()
        y_out[:, across(h)] = both_cores(1 - run, h).astype(jnp.bfloat16)
        y_copy(h).start()

    def basis_slot(place, h):
        return out_ref.at[place * 2 + x, core, :, across(h)]

    def basis_x(place, side, h):
        ref = out_ref.at[place * 2 + side, core, :, across(h)]
        return pltpu.make_async_remote_copy(
            src_ref=ref, dst_ref=ref, send_sem=bx_send.at[place, h],
            recv_sem=bx_recv.at[place, h], device_id=to_x, device_id_type=MESH)

    def basis_core(at, who, h):
        ref = out_ref.at[at, who, :, across(h)]
        return pltpu.make_async_remote_copy(
            src_ref=ref, dst_ref=ref, send_sem=bc_send.at[at, h],
            recv_sem=bc_recv.at[at, h], device_id=to_core, device_id_type=MESH)

    def basis_begin(h):
        y_copy(h).wait_recv()
        both = both_cores(run, h) + y_in[:, across(h)].astype(jnp.float32)
        out_ref[tm, core, :, across(h)] = both.astype(jnp.bfloat16)

    def basis_ready(place, h):
        basis_x(place, x, h).start()
        basis_core(place * 2 + x, core, h).start()

    basis_sends = line_gather(
        n_z, z, range(2), basis_slot, to_up, to_down, basis_begin, basis_ready, lambda: None,
        (b_up, b_down, b_recv))
    for place in (z, pair, 2 - far, 3 - 3 * far):
        for h in range(2):
            basis_x(place, 1 - x, h).wait_recv()
            basis_core(place * 2 + 1 - x, core, h).start()
    for h in range(2):
        for at in range(n_time):
            basis_core(at, 1 - core, h).wait_recv()
    frame_copy(run).wait_send()
    for k in chunks:
        for place in range(n_z):
            unless_by_pair(place, k, lambda: panel_x(place, x, k).wait_send())
    for k in by_pair:
        panel_pair(z, k).wait_send()
    panel_sends()
    basis_sends()
    for h in range(2):
        core_copy(h).wait_send()
        y_copy(h).wait_send()
        for place in range(n_z):
            basis_x(place, x, h).wait_send()
        for at in range(n_time):
            basis_core(at, core, h).wait_send()


def gathered_basis(frames, low, high, n_time):
    t_local, features = frames.shape
    width = 2 * low.shape[0] * n_time
    n_z = n_time // 2
    half = t_local // 2
    dma = pltpu.SemaphoreType.DMA
    vmem = pltpu.VMEM
    flops = 2 * t_local * features * width
    return pl.pallas_call(
        functools.partial(kernel, n_time),
        out_shape=jax.ShapeDtypeStruct((n_time, 2, half, width), jnp.bfloat16),
        in_specs=[pl.BlockSpec(memory_space=pl.ANY)] * 3,
        out_specs=pl.BlockSpec(memory_space=pltpu.VMEM),
        scratch_shapes=[
            vmem((2, t_local, features // 2), jnp.bfloat16),
            vmem((2, n_time, low.shape[0], features // 2), jnp.bfloat16),
            vmem((2 * t_local, width), jnp.float32),
            vmem((2, 2, half, width), jnp.bfloat16),
            vmem((2, half, width), jnp.bfloat16),
            vmem((half, width), jnp.bfloat16),
            vmem((half, width), jnp.bfloat16),
            dma((3,)), dma((1,)), dma((1,)),
            *[dma((n_z, 4))] * 5, dma((4,)), dma((4,)),
            *[dma((2,))] * 4,
            *[dma((n_z, 2))] * 5, dma((n_time, 2)), dma((n_time, 2)),
        ],
        compiler_params=pltpu.CompilerParams(
            collective_id=0, has_side_effects=True, vmem_limit_bytes=56 * 2**20),
        cost_estimate=pl.CostEstimate(flops=flops, bytes_accessed=16 * 2**20, transcendentals=0),
    )(frames, low, high)


def local(frames, panel_low, panel_high, lags, seg_lengths, ridge):
    t_local = frames.shape[1]
    n_time = lax.axis_size("tm")
    tm, core, run = lax.axis_index("tm"), lax.axis_index("feat"), lax.axis_index("rep")
    basis = gathered_basis(frames[0], panel_low.T, panel_high.T, n_time)
    width = basis.shape[-1]
    total = t_local * n_time
    basis = basis.reshape(total, width)
    rows = width // (n_time * 2)
    lag_most = t_local // 4
    lag_now = lags[0]
    positions = jnp.arange(total, dtype=jnp.int32)
    seg_ends = jnp.cumsum(seg_lengths[0])
    end_of = jnp.min(
        jnp.where(seg_ends[None, :] > positions[:, None], seg_ends[None, :], total), axis=1
    )
    keep = (positions + lag_now < end_of).astype(jnp.bfloat16)

    def later(values):
        spare = jnp.zeros((lag_most,) + values.shape[1:], values.dtype)
        return lax.dynamic_slice_in_dim(
            jnp.concatenate([spare, values], axis=0), lag_most - lag_now, total, 0)

    later_keep = later(keep)
    first = (tm * 2 + core) * rows
    own = lax.dynamic_slice(basis, (0, first), (total, rows))
    masked = own * keep[:, None]
    left = jnp.concatenate([masked, later(masked), own * later_keep[:, None]], axis=1)
    terms = jnp.einsum("ta,tj->aj", left, basis, preferred_element_type=jnp.float32)
    terms = terms.reshape(3, 2, rows // 2, width)
    variance = jnp.sum(
        jnp.square(basis.astype(jnp.float32)) * later_keep.astype(jnp.float32)[:, None], axis=0,
        keepdims=True)
    theirs = lax.dynamic_index_in_dim(terms, 1 - run, 1, keepdims=False).reshape(-1, width)
    mine = lax.dynamic_index_in_dim(terms, run, 1, keepdims=False)
    received = lax.ppermute(
        jnp.concatenate([theirs, variance], axis=0), "rep", [(0, 1), (1, 0)])
    inverse_count = 1.0 / (total * 2)
    cov_rows = (mine + received[:-1].reshape(mine.shape)) * inverse_count
    diag_lagged = (variance[0] + received[-1]) * inverse_count
    return finish(cov_rows, diag_lagged, ridge)


def solution(mesh):
    in_specs = (
        P("rep", "tm", "feat"),
        P("feat", "tm"),
        P("feat", "tm"),
        P("rep"),
        P("rep", None),
        P(),
    )
    out_specs = (P(None, ("tm", "feat", "rep"), None), P(("tm", "feat", "rep"), None))
    shape = dict(mesh.shape)
    paired = shape["feat"] == 2 and shape["rep"] == 2 and shape["tm"] == 8
    body = local if paired else local_general
    return jax.shard_map(body, mesh=mesh, in_specs=in_specs, out_specs=out_specs, check_vma=False)
```

```python
import functools
import jax
import jax.numpy as jnp
from jax import lax
from jax.experimental import pallas as pl
from jax.experimental.pallas import tpu as pltpu
from jax.sharding import PartitionSpec as P

MESH = pl.DeviceIdType.MESH
N_CHUNK = 8
TILE = 1024


def passed_along(shard, axis, by):
    length = lax.axis_size(axis)
    pairs = [(i, i + by) for i in range(length) if 0 <= i + by < length]
    return lax.ppermute(shard, axis, pairs)


def local_general(frames, panel_low, panel_high, lags, seg_lengths, ridge):
    local_frames = frames[0]
    t_local = local_frames.shape[0]
    lag_most = t_local // 4
    n_time = lax.axis_size("tm")
    n_feature = lax.axis_size("feat")
    n_replica = lax.axis_size("rep")
    panel_cols = panel_low.shape[1] * n_time
    basis_width = 2 * panel_cols
    per_device = basis_width // (n_time * n_feature * n_replica)
    time_index = lax.axis_index("tm")
    feature_index = lax.axis_index("feat")
    replica_index = lax.axis_index("rep")
    stacked = jnp.stack([panel_low, panel_high], axis=0)
    partial_sum = jnp.einsum(
        "tf,pfk->tpk",
        local_frames,
        lax.all_gather(stacked, "tm", axis=2, tiled=True),
        preferred_element_type=jnp.float32,
    )
    partial_sum = partial_sum.reshape(local_frames.shape[0], basis_width)
    partial_rounded = partial_sum.astype(jnp.bfloat16)
    summed = lax.psum(partial_rounded, "feat").astype(jnp.float32).astype(jnp.bfloat16)
    next_basis = passed_along(summed[:lag_most], "tm", -1)
    extended = jnp.concatenate([summed, next_basis], axis=0)
    lag_now = lags[0]
    lagged = lax.dynamic_slice_in_dim(extended, lag_now, t_local, 0)
    frame_total = t_local * n_time
    positions = time_index * t_local + jnp.arange(t_local, dtype=jnp.int32)
    seg_ends = jnp.cumsum(seg_lengths[0])
    end_of = jnp.min(
        jnp.where(seg_ends[None, :] > positions[:, None], seg_ends[None, :], frame_total), axis=1
    )
    keep_mask = (positions + lag_now < end_of).astype(jnp.bfloat16)[:, None]
    masked = summed * keep_mask
    lag_masked = lagged * keep_mask

    def own_group(values):
        shaped = values.reshape(t_local, n_time, n_feature, n_replica * per_device)
        return lax.dynamic_index_in_dim(shaped, feature_index, 2, keepdims=False).reshape(
            t_local, -1
        )

    group_masked = own_group(masked)
    group_lagged = own_group(lag_masked)
    term_inst = jnp.einsum("ti,tj->ij", group_masked, summed, preferred_element_type=jnp.float32)
    term_cross = jnp.einsum("ti,tj->ij", group_masked, lagged, preferred_element_type=jnp.float32)
    term_lagged = jnp.einsum("ti,tj->ij", group_lagged, lagged, preferred_element_type=jnp.float32)
    row_block = lax.psum_scatter(
        jnp.stack([term_inst, term_cross, term_lagged], axis=1),
        ("tm", "rep"),
        scatter_dimension=0,
        tiled=True,
    )
    inverse_count = 1.0 / (frame_total * n_replica)
    cov_rows = jnp.transpose(row_block, (1, 0, 2)) * inverse_count
    local_var = jnp.sum(jnp.square(lag_masked.astype(jnp.float32)), axis=0)
    diag_lagged = lax.psum(local_var, ("tm", "rep")) * inverse_count
    return finish(cov_rows, diag_lagged, ridge)


def finish(cov_rows, diag_lagged, ridge):
    per_device, basis_width = cov_rows.shape[1:]
    device_linear = (
        lax.axis_index("tm") * lax.axis_size("feat") + lax.axis_index("feat")
    ) * lax.axis_size("rep") + lax.axis_index("rep")
    own_index = device_linear * per_device + jnp.arange(per_device, dtype=jnp.int32)
    selector = (jnp.arange(basis_width, dtype=jnp.int32)[None, :] == own_index[:, None]).astype(
        jnp.float32
    )
    diag_inst = jnp.sum(cov_rows[0] * selector, axis=1)
    inverse_lagged = 1.0 / (diag_lagged[:, None] + ridge[None, :])
    weighted = jnp.dot(
        jnp.square(cov_rows[1]),
        inverse_lagged,
        precision=lax.Precision.HIGHEST,
        preferred_element_type=jnp.float32,
    )
    scores = weighted / (diag_inst[:, None] + ridge[None, :])
    return (cov_rows, scores)


def line_gather(n_z, z, chunks, slot, send_up, send_down, begin, ready, at_end, sems):
    up_sem, down_sem, recv_sem = sems

    def copy(place, k, sem, target):
        return pltpu.make_async_remote_copy(
            src_ref=slot(place, k), dst_ref=slot(place, k), send_sem=sem.at[place, k],
            recv_sem=recv_sem.at[place, k], device_id=target, device_id_type=MESH)

    for k in chunks:
        begin(k)

        @pl.when(z + 1 < n_z)
        def _():
            copy(z, k, up_sem, send_up).start()

        @pl.when(z > 0)
        def _():
            copy(z, k, down_sem, send_down).start()

        ready(z, k)
    for step in range(1, n_z):
        for k in chunks:
            @pl.when(z - step >= 0)
            def _():
                place = z - step
                copy(place, k, up_sem, send_up).wait_recv()

                @pl.when(z + 1 < n_z)
                def _():
                    copy(place, k, up_sem, send_up).start()

                ready(place, k)

            @pl.when(z + step < n_z)
            def _():
                place = z + step
                copy(place, k, down_sem, send_down).wait_recv()

                @pl.when(z > 0)
                def _():
                    copy(place, k, down_sem, send_down).start()

                ready(place, k)

    at_end()

    def finish_sends():
        for place in range(n_z):
            for k in chunks:
                @pl.when(jnp.logical_and(z + 1 < n_z, place <= z))
                def _():
                    copy(place, k, up_sem, send_up).wait_send()

                @pl.when(jnp.logical_and(z > 0, place >= z))
                def _():
                    copy(place, k, down_sem, send_down).wait_send()

    return finish_sends


def kernel(n_time, frames_ref, low_ref, high_ref, out_ref, all_frames, all_panels, total, part, other,
           y_out, y_in, local_sem, f_send, f_recv, p_up, p_down, p_recv, px_send, px_recv,
           pz_send, pz_recv, c_send, c_recv, y_send, y_recv,
           b_up, b_down, b_recv, bx_send, bx_recv, bc_send, bc_recv):
    n_z = n_time // 2
    tm, core, run = lax.axis_index("tm"), lax.axis_index("feat"), lax.axis_index("rep")
    z, x = tm // 2, tm % 2
    pair = z + 1 - 2 * (z % 2)
    to_up = (jnp.minimum(tm + 2, n_time - 2 + x), core, run)
    to_down = (jnp.maximum(tm - 2, x), core, run)
    to_pair = (pair * 2 + x, core, run)
    to_x = (z * 2 + (1 - x), core, run)
    to_y = (tm, core, 1 - run)
    to_core = (tm, 1 - core, run)
    features = all_frames.shape[2]
    cut = features // (N_CHUNK // 2)
    chunks = range(N_CHUNK)
    by_pair = range(N_CHUNK // 2, N_CHUNK)

    own_lanes = pl.ds(pl.multiple_of(run * features, features), features)
    their_lanes = pl.ds(pl.multiple_of((1 - run) * features, features), features)
    own_low = pltpu.make_async_copy(low_ref.at[:, own_lanes], all_panels.at[0, tm], local_sem.at[0])
    own_high = pltpu.make_async_copy(high_ref.at[:, own_lanes], all_panels.at[1, tm], local_sem.at[1])
    own_frames = pltpu.make_async_copy(
        frames_ref.at[:, own_lanes], all_frames.at[run], local_sem.at[2])
    own_low.start()
    own_high.start()
    own_frames.start()

    barrier = pltpu.get_barrier_semaphore()

    @pl.when(z + 1 < n_z)
    def _():
        pl.semaphore_signal(barrier, inc=1, device_id=to_up, device_id_type=MESH)

    @pl.when(z > 0)
    def _():
        pl.semaphore_signal(barrier, inc=1, device_id=to_down, device_id_type=MESH)

    for target in (to_x, to_y, to_core):
        pl.semaphore_signal(barrier, inc=1, device_id=target, device_id_type=MESH)

    @pl.when(jnp.logical_or(z == 0, z == n_z - 1))
    def _():
        pl.semaphore_wait(barrier, 4)

    @pl.when(jnp.logical_and(z > 0, z < n_z - 1))
    def _():
        pl.semaphore_wait(barrier, 5)

    def frame_copy(slot_run):
        return pltpu.make_async_remote_copy(
            src_ref=frames_ref.at[:, their_lanes], dst_ref=all_frames.at[slot_run],
            send_sem=f_send.at[0], recv_sem=f_recv.at[0], device_id=to_y, device_id_type=MESH)

    def panel_ref(place, side, k):
        return all_panels.at[
            k // (N_CHUNK // 2), place * 2 + side, :, pl.ds(k % (N_CHUNK // 2) * cut, cut)]

    def panel_slot(place, k):
        return panel_ref(place, x, k)

    def panel_x(place, side, k):
        ref = panel_ref(place, side, k)
        return pltpu.make_async_remote_copy(
            src_ref=ref, dst_ref=ref, send_sem=px_send.at[place, k],
            recv_sem=px_recv.at[place, k], device_id=to_x, device_id_type=MESH)

    def panel_pair(place, k):
        ref = panel_ref(place, 1 - x, k)
        return pltpu.make_async_remote_copy(
            src_ref=ref, dst_ref=ref, send_sem=pz_send.at[k], recv_sem=pz_recv.at[k],
            device_id=to_pair, device_id_type=MESH)

    def unless_by_pair(place, k, act):
        if k in by_pair:
            pl.when(place != pair)(act)
        else:
            act()

    def panel_begin(k):
        if k == 0:
            own_low.wait()
        if k == N_CHUNK // 2:
            own_high.wait()

    def panel_ready(place, k):
        unless_by_pair(place, k, lambda: panel_x(place, x, k).start())

    def pass_to_pair():
        for k in by_pair:
            panel_x(z, 1 - x, k).wait_recv()
            panel_pair(z, k).start()

    frame_copy(run).start()
    panel_sends = line_gather(
        n_z, z, chunks, panel_slot, to_up, to_down, panel_begin, panel_ready, pass_to_pair,
        (p_up, p_down, p_recv))
    own_frames.wait()
    frame_copy(1 - run).wait_recv()
    far = z // 2
    rows, columns = total.shape
    block = all_panels.shape[2] * 2
    for turn, place in enumerate((z, 2 - far, 3 - 3 * far, pair)):
        for k in chunks:
            if turn == 0 and k in by_pair:
                continue
            if turn == 3 and k in by_pair:
                panel_pair(place, k).wait_recv()
            else:
                panel_x(place, 1 - x, k).wait_recv()

        def term(i, so_far):
            at = pl.ds(pl.multiple_of(i * TILE, TILE), TILE)
            left = all_frames[:, :, at].reshape(rows, TILE)
            right = all_panels[:, pl.ds(place * 2, 2), :, at].reshape(2 * block, TILE)
            return so_far + lax.dot_general(
                left, right, (((1,), (1,)), ((), ())), preferred_element_type=jnp.float32)

        result = lax.fori_loop(
            0, features // TILE, term, jnp.zeros((rows, 2 * block), jnp.float32))
        for panel in range(2):
            at = pl.ds(pl.multiple_of(panel * (columns // 2) + place * block, block), block)
            total[:, at] = result[:, panel * block:(panel + 1) * block]
            part[:, :, :, at] = result[:, panel * block:(panel + 1) * block].astype(
                jnp.bfloat16).reshape(2, 2, rows // 4, block)

    half = rows // 4
    wide = columns // 2
    own_rows = pl.multiple_of(core * half, half)

    def across(h):
        return pl.ds(h * wide, wide)

    def core_copy(h):
        return pltpu.make_async_remote_copy(
            src_ref=part.at[:, 1 - core, :, across(h)], dst_ref=other.at[:, :, across(h)],
            send_sem=c_send.at[h], recv_sem=c_recv.at[h], device_id=to_core, device_id_type=MESH)

    def y_copy(h):
        return pltpu.make_async_remote_copy(
            src_ref=y_out.at[:, across(h)], dst_ref=y_in.at[:, across(h)],
            send_sem=y_send.at[h], recv_sem=y_recv.at[h], device_id=to_y, device_id_type=MESH)

    def both_cores(which, h):
        first = pl.multiple_of(which * 2 * half + own_rows, half)
        return total[pl.ds(first, half), across(h)] + other[which, :, across(h)].astype(jnp.float32)

    for h in range(2):
        core_copy(h).start()
    for h in range(2):
        core_copy(h).wait_recv()
        y_out[:, across(h)] = both_cores(1 - run, h).astype(jnp.bfloat16)
        y_copy(h).start()

    def basis_slot(place, h):
        return out_ref.at[place * 2 + x, core, :, across(h)]

    def basis_x(place, side, h):
        ref = out_ref.at[place * 2 + side, core, :, across(h)]
        return pltpu.make_async_remote_copy(
            src_ref=ref, dst_ref=ref, send_sem=bx_send.at[place, h],
            recv_sem=bx_recv.at[place, h], device_id=to_x, device_id_type=MESH)

    def basis_core(at, who, h):
        ref = out_ref.at[at, who, :, across(h)]
        return pltpu.make_async_remote_copy(
            src_ref=ref, dst_ref=ref, send_sem=bc_send.at[at, h],
            recv_sem=bc_recv.at[at, h], device_id=to_core, device_id_type=MESH)

    def basis_begin(h):
        y_copy(h).wait_recv()
        both = both_cores(run, h) + y_in[:, across(h)].astype(jnp.float32)
        out_ref[tm, core, :, across(h)] = both.astype(jnp.bfloat16)

    def basis_ready(place, h):
        basis_x(place, x, h).start()
        basis_core(place * 2 + x, core, h).start()

    basis_sends = line_gather(
        n_z, z, range(2), basis_slot, to_up, to_down, basis_begin, basis_ready, lambda: None,
        (b_up, b_down, b_recv))
    for place in (z, pair, 2 - far, 3 - 3 * far):
        for h in range(2):
            basis_x(place, 1 - x, h).wait_recv()
            basis_core(place * 2 + 1 - x, core, h).start()
    for h in range(2):
        for at in range(n_time):
            basis_core(at, 1 - core, h).wait_recv()
    frame_copy(run).wait_send()
    for k in chunks:
        for place in range(n_z):
            unless_by_pair(place, k, lambda: panel_x(place, x, k).wait_send())
    for k in by_pair:
        panel_pair(z, k).wait_send()
    panel_sends()
    basis_sends()
    for h in range(2):
        core_copy(h).wait_send()
        y_copy(h).wait_send()
        for place in range(n_z):
            basis_x(place, x, h).wait_send()
        for at in range(n_time):
            basis_core(at, core, h).wait_send()


def gathered_basis(frames, low, high, n_time):
    t_local, features = frames.shape
    width = 2 * low.shape[0] * n_time
    n_z = n_time // 2
    half = t_local // 2
    dma = pltpu.SemaphoreType.DMA
    vmem = pltpu.VMEM
    flops = 2 * t_local * features * width
    return pl.pallas_call(
        functools.partial(kernel, n_time),
        out_shape=jax.ShapeDtypeStruct((n_time, 2, half, width), jnp.bfloat16),
        in_specs=[pl.BlockSpec(memory_space=pl.ANY)] * 3,
        out_specs=pl.BlockSpec(memory_space=pltpu.VMEM),
        scratch_shapes=[
            vmem((2, t_local, features // 2), jnp.bfloat16),
            vmem((2, n_time, low.shape[0], features // 2), jnp.bfloat16),
            vmem((2 * t_local, width), jnp.float32),
            vmem((2, 2, half, width), jnp.bfloat16),
            vmem((2, half, width), jnp.bfloat16),
            vmem((half, width), jnp.bfloat16),
            vmem((half, width), jnp.bfloat16),
            dma((3,)), dma((1,)), dma((1,)),
            *[dma((n_z, N_CHUNK))] * 5, dma((N_CHUNK,)), dma((N_CHUNK,)),
            *[dma((2,))] * 4,
            *[dma((n_z, 2))] * 5, dma((n_time, 2)), dma((n_time, 2)),
        ],
        compiler_params=pltpu.CompilerParams(
            collective_id=0, has_side_effects=True, vmem_limit_bytes=56 * 2**20),
        cost_estimate=pl.CostEstimate(flops=flops, bytes_accessed=16 * 2**20, transcendentals=0),
    )(frames, low, high)


def local(frames, panel_low, panel_high, lags, seg_lengths, ridge):
    t_local = frames.shape[1]
    n_time = lax.axis_size("tm")
    tm, core, run = lax.axis_index("tm"), lax.axis_index("feat"), lax.axis_index("rep")
    basis = gathered_basis(frames[0], panel_low.T, panel_high.T, n_time)
    width = basis.shape[-1]
    total = t_local * n_time
    basis = basis.reshape(total, width)
    rows = width // (n_time * 2)
    lag_most = t_local // 4
    lag_now = lags[0]
    positions = jnp.arange(total, dtype=jnp.int32)
    seg_ends = jnp.cumsum(seg_lengths[0])
    end_of = jnp.min(
        jnp.where(seg_ends[None, :] > positions[:, None], seg_ends[None, :], total), axis=1
    )
    keep = (positions + lag_now < end_of).astype(jnp.bfloat16)

    def later(values):
        spare = jnp.zeros((lag_most,) + values.shape[1:], values.dtype)
        return lax.dynamic_slice_in_dim(
            jnp.concatenate([spare, values], axis=0), lag_most - lag_now, total, 0)

    later_keep = later(keep)
    first = (tm * 2 + core) * rows
    own = lax.dynamic_slice(basis, (0, first), (total, rows))
    masked = own * keep[:, None]
    left = jnp.concatenate([masked, later(masked), own * later_keep[:, None]], axis=1)
    terms = jnp.einsum("ta,tj->aj", left, basis, preferred_element_type=jnp.float32)
    terms = terms.reshape(3, 2, rows // 2, width)
    variance = jnp.sum(
        jnp.square(basis.astype(jnp.float32)) * later_keep.astype(jnp.float32)[:, None], axis=0,
        keepdims=True)
    theirs = lax.dynamic_index_in_dim(terms, 1 - run, 1, keepdims=False).reshape(-1, width)
    mine = lax.dynamic_index_in_dim(terms, run, 1, keepdims=False)
    swap = [(0, 1), (1, 0)]
    received = lax.ppermute(theirs, "rep", swap)
    other_variance = lax.ppermute(variance, "rep", swap)
    inverse_count = 1.0 / (total * 2)
    cov_rows = (mine + received.reshape(mine.shape)) * inverse_count
    diag_lagged = (variance + other_variance)[0] * inverse_count
    return finish(cov_rows, diag_lagged, ridge)


def solution(mesh):
    in_specs = (
        P("rep", "tm", "feat"),
        P("feat", "tm"),
        P("feat", "tm"),
        P("rep"),
        P("rep", None),
        P(),
    )
    out_specs = (P(None, ("tm", "feat", "rep"), None), P(("tm", "feat", "rep"), None))
    shape = dict(mesh.shape)
    paired = shape["feat"] == 2 and shape["rep"] == 2 and shape["tm"] == 8
    body = local if paired else local_general
    return jax.shard_map(body, mesh=mesh, in_specs=in_specs, out_specs=out_specs, check_vma=False)
```

```python
import functools
import jax
import jax.numpy as jnp
from jax import lax
from jax.experimental import pallas as pl
from jax.experimental.pallas import tpu as pltpu
from jax.sharding import PartitionSpec as P

MESH = pl.DeviceIdType.MESH
N_CHUNK = 8
N_PIECE = 4
TILE = 1024


def passed_along(shard, axis, by):
    length = lax.axis_size(axis)
    pairs = [(i, i + by) for i in range(length) if 0 <= i + by < length]
    return lax.ppermute(shard, axis, pairs)


def local_general(frames, panel_low, panel_high, lags, seg_lengths, ridge):
    local_frames = frames[0]
    t_local = local_frames.shape[0]
    lag_most = t_local // 4
    n_time = lax.axis_size("tm")
    n_feature = lax.axis_size("feat")
    n_replica = lax.axis_size("rep")
    panel_cols = panel_low.shape[1] * n_time
    basis_width = 2 * panel_cols
    per_device = basis_width // (n_time * n_feature * n_replica)
    time_index = lax.axis_index("tm")
    feature_index = lax.axis_index("feat")
    replica_index = lax.axis_index("rep")
    stacked = jnp.stack([panel_low, panel_high], axis=0)
    partial_sum = jnp.einsum(
        "tf,pfk->tpk",
        local_frames,
        lax.all_gather(stacked, "tm", axis=2, tiled=True),
        preferred_element_type=jnp.float32,
    )
    partial_sum = partial_sum.reshape(local_frames.shape[0], basis_width)
    partial_rounded = partial_sum.astype(jnp.bfloat16)
    summed = lax.psum(partial_rounded, "feat").astype(jnp.float32).astype(jnp.bfloat16)
    next_basis = passed_along(summed[:lag_most], "tm", -1)
    extended = jnp.concatenate([summed, next_basis], axis=0)
    lag_now = lags[0]
    lagged = lax.dynamic_slice_in_dim(extended, lag_now, t_local, 0)
    frame_total = t_local * n_time
    positions = time_index * t_local + jnp.arange(t_local, dtype=jnp.int32)
    seg_ends = jnp.cumsum(seg_lengths[0])
    end_of = jnp.min(
        jnp.where(seg_ends[None, :] > positions[:, None], seg_ends[None, :], frame_total), axis=1
    )
    keep_mask = (positions + lag_now < end_of).astype(jnp.bfloat16)[:, None]
    masked = summed * keep_mask
    lag_masked = lagged * keep_mask

    def own_group(values):
        shaped = values.reshape(t_local, n_time, n_feature, n_replica * per_device)
        return lax.dynamic_index_in_dim(shaped, feature_index, 2, keepdims=False).reshape(
            t_local, -1
        )

    group_masked = own_group(masked)
    group_lagged = own_group(lag_masked)
    term_inst = jnp.einsum("ti,tj->ij", group_masked, summed, preferred_element_type=jnp.float32)
    term_cross = jnp.einsum("ti,tj->ij", group_masked, lagged, preferred_element_type=jnp.float32)
    term_lagged = jnp.einsum("ti,tj->ij", group_lagged, lagged, preferred_element_type=jnp.float32)
    row_block = lax.psum_scatter(
        jnp.stack([term_inst, term_cross, term_lagged], axis=1),
        ("tm", "rep"),
        scatter_dimension=0,
        tiled=True,
    )
    inverse_count = 1.0 / (frame_total * n_replica)
    cov_rows = jnp.transpose(row_block, (1, 0, 2)) * inverse_count
    local_var = jnp.sum(jnp.square(lag_masked.astype(jnp.float32)), axis=0)
    diag_lagged = lax.psum(local_var, ("tm", "rep")) * inverse_count
    return finish(cov_rows, diag_lagged, ridge)


def finish(cov_rows, diag_lagged, ridge):
    per_device, basis_width = cov_rows.shape[1:]
    device_linear = (
        lax.axis_index("tm") * lax.axis_size("feat") + lax.axis_index("feat")
    ) * lax.axis_size("rep") + lax.axis_index("rep")
    own_index = device_linear * per_device + jnp.arange(per_device, dtype=jnp.int32)
    selector = (jnp.arange(basis_width, dtype=jnp.int32)[None, :] == own_index[:, None]).astype(
        jnp.float32
    )
    diag_inst = jnp.sum(cov_rows[0] * selector, axis=1)
    inverse_lagged = 1.0 / (diag_lagged[:, None] + ridge[None, :])
    weighted = jnp.dot(
        jnp.square(cov_rows[1]),
        inverse_lagged,
        precision=lax.Precision.HIGHEST,
        preferred_element_type=jnp.float32,
    )
    scores = weighted / (diag_inst[:, None] + ridge[None, :])
    return (cov_rows, scores)


def line_gather(n_z, z, chunks, slot, send_up, send_down, begin, ready, at_end, sems):
    up_sem, down_sem, recv_sem = sems

    def copy(place, k, sem, target):
        return pltpu.make_async_remote_copy(
            src_ref=slot(place, k), dst_ref=slot(place, k), send_sem=sem.at[place, k],
            recv_sem=recv_sem.at[place, k], device_id=target, device_id_type=MESH)

    for k in chunks:
        begin(k)

        @pl.when(z + 1 < n_z)
        def _():
            copy(z, k, up_sem, send_up).start()

        @pl.when(z > 0)
        def _():
            copy(z, k, down_sem, send_down).start()

        ready(z, k)
    for step in range(1, n_z):
        for k in chunks:
            @pl.when(z - step >= 0)
            def _():
                place = z - step
                copy(place, k, up_sem, send_up).wait_recv()

                @pl.when(z + 1 < n_z)
                def _():
                    copy(place, k, up_sem, send_up).start()

                ready(place, k)

            @pl.when(z + step < n_z)
            def _():
                place = z + step
                copy(place, k, down_sem, send_down).wait_recv()

                @pl.when(z > 0)
                def _():
                    copy(place, k, down_sem, send_down).start()

                ready(place, k)

    at_end()

    def finish_sends():
        for place in range(n_z):
            for k in chunks:
                @pl.when(jnp.logical_and(z + 1 < n_z, place <= z))
                def _():
                    copy(place, k, up_sem, send_up).wait_send()

                @pl.when(jnp.logical_and(z > 0, place >= z))
                def _():
                    copy(place, k, down_sem, send_down).wait_send()

    return finish_sends


def kernel(n_time, frames_ref, low_ref, high_ref, out_ref, all_frames, all_panels, total, part, other,
           y_out, y_in, local_sem, f_send, f_recv, p_up, p_down, p_recv, px_send, px_recv,
           pz_send, pz_recv, c_send, c_recv, y_send, y_recv,
           b_up, b_down, b_recv, bx_send, bx_recv, bc_send, bc_recv, bz_send, bz_recv):
    n_z = n_time // 2
    tm, core, run = lax.axis_index("tm"), lax.axis_index("feat"), lax.axis_index("rep")
    z, x = tm // 2, tm % 2
    pair = z + 1 - 2 * (z % 2)
    to_up = (jnp.minimum(tm + 2, n_time - 2 + x), core, run)
    to_down = (jnp.maximum(tm - 2, x), core, run)
    to_pair = (pair * 2 + x, core, run)
    to_x = (z * 2 + (1 - x), core, run)
    to_y = (tm, core, 1 - run)
    to_core = (tm, 1 - core, run)
    features = all_frames.shape[2]
    cut = features // (N_CHUNK // 2)
    chunks = range(N_CHUNK)
    by_pair = range(N_CHUNK // 2, N_CHUNK)

    own_lanes = pl.ds(pl.multiple_of(run * features, features), features)
    their_lanes = pl.ds(pl.multiple_of((1 - run) * features, features), features)
    own_low = pltpu.make_async_copy(low_ref.at[:, own_lanes], all_panels.at[0, tm], local_sem.at[0])
    own_high = pltpu.make_async_copy(high_ref.at[:, own_lanes], all_panels.at[1, tm], local_sem.at[1])
    own_frames = pltpu.make_async_copy(
        frames_ref.at[:, own_lanes], all_frames.at[run], local_sem.at[2])
    own_low.start()
    own_high.start()
    own_frames.start()

    barrier = pltpu.get_barrier_semaphore()

    @pl.when(z + 1 < n_z)
    def _():
        pl.semaphore_signal(barrier, inc=1, device_id=to_up, device_id_type=MESH)

    @pl.when(z > 0)
    def _():
        pl.semaphore_signal(barrier, inc=1, device_id=to_down, device_id_type=MESH)

    for target in (to_x, to_y, to_core):
        pl.semaphore_signal(barrier, inc=1, device_id=target, device_id_type=MESH)

    @pl.when(jnp.logical_or(z == 0, z == n_z - 1))
    def _():
        pl.semaphore_wait(barrier, 4)

    @pl.when(jnp.logical_and(z > 0, z < n_z - 1))
    def _():
        pl.semaphore_wait(barrier, 5)

    def frame_copy(slot_run):
        return pltpu.make_async_remote_copy(
            src_ref=frames_ref.at[:, their_lanes], dst_ref=all_frames.at[slot_run],
            send_sem=f_send.at[0], recv_sem=f_recv.at[0], device_id=to_y, device_id_type=MESH)

    def panel_ref(place, side, k):
        return all_panels.at[
            k // (N_CHUNK // 2), place * 2 + side, :, pl.ds(k % (N_CHUNK // 2) * cut, cut)]

    def panel_slot(place, k):
        return panel_ref(place, x, k)

    def panel_x(place, side, k):
        ref = panel_ref(place, side, k)
        return pltpu.make_async_remote_copy(
            src_ref=ref, dst_ref=ref, send_sem=px_send.at[place, k],
            recv_sem=px_recv.at[place, k], device_id=to_x, device_id_type=MESH)

    def panel_pair(place, k):
        ref = panel_ref(place, 1 - x, k)
        return pltpu.make_async_remote_copy(
            src_ref=ref, dst_ref=ref, send_sem=pz_send.at[k], recv_sem=pz_recv.at[k],
            device_id=to_pair, device_id_type=MESH)

    def unless_by_pair(place, k, act, passed=by_pair):
        if k in passed:
            pl.when(place != pair)(act)
        else:
            act()

    def panel_begin(k):
        if k == 0:
            own_low.wait()
        if k == N_CHUNK // 2:
            own_high.wait()

    def panel_ready(place, k):
        unless_by_pair(place, k, lambda: panel_x(place, x, k).start())

    def pass_to_pair():
        for k in by_pair:
            panel_x(z, 1 - x, k).wait_recv()
            panel_pair(z, k).start()

    frame_copy(run).start()
    panel_sends = line_gather(
        n_z, z, chunks, panel_slot, to_up, to_down, panel_begin, panel_ready, pass_to_pair,
        (p_up, p_down, p_recv))
    own_frames.wait()
    frame_copy(1 - run).wait_recv()
    far = z // 2
    rows, columns = total.shape
    block = all_panels.shape[2] * 2
    for turn, place in enumerate((z, 2 - far, 3 - 3 * far, pair)):
        for k in chunks:
            if turn == 0 and k in by_pair:
                continue
            if turn == 3 and k in by_pair:
                panel_pair(place, k).wait_recv()
            else:
                panel_x(place, 1 - x, k).wait_recv()

        def term(i, so_far):
            at = pl.ds(pl.multiple_of(i * TILE, TILE), TILE)
            left = all_frames[:, :, at].reshape(rows, TILE)
            right = all_panels[:, pl.ds(place * 2, 2), :, at].reshape(2 * block, TILE)
            return so_far + lax.dot_general(
                left, right, (((1,), (1,)), ((), ())), preferred_element_type=jnp.float32)

        result = lax.fori_loop(
            0, features // TILE, term, jnp.zeros((rows, 2 * block), jnp.float32))
        for panel in range(2):
            at = pl.ds(pl.multiple_of(panel * (columns // 2) + place * block, block), block)
            total[:, at] = result[:, panel * block:(panel + 1) * block]
            part[:, :, :, at] = result[:, panel * block:(panel + 1) * block].astype(
                jnp.bfloat16).reshape(2, 2, rows // 4, block)

    half = rows // 4
    wide = columns // N_PIECE
    pieces = range(N_PIECE)
    late = range(N_PIECE // 2, N_PIECE)
    own_rows = pl.multiple_of(core * half, half)

    def across(h):
        return pl.ds(h * wide, wide)

    def core_copy(h):
        return pltpu.make_async_remote_copy(
            src_ref=part.at[:, 1 - core, :, across(h)], dst_ref=other.at[:, :, across(h)],
            send_sem=c_send.at[h], recv_sem=c_recv.at[h], device_id=to_core, device_id_type=MESH)

    def y_copy(h):
        return pltpu.make_async_remote_copy(
            src_ref=y_out.at[:, across(h)], dst_ref=y_in.at[:, across(h)],
            send_sem=y_send.at[h], recv_sem=y_recv.at[h], device_id=to_y, device_id_type=MESH)

    def both_cores(which, h):
        first = pl.multiple_of(which * 2 * half + own_rows, half)
        return total[pl.ds(first, half), across(h)] + other[which, :, across(h)].astype(jnp.float32)

    for h in pieces:
        core_copy(h).start()
    for h in pieces:
        core_copy(h).wait_recv()
        y_out[:, across(h)] = both_cores(1 - run, h).astype(jnp.bfloat16)
        y_copy(h).start()

    def basis_slot(place, h):
        return out_ref.at[place * 2 + x, core, :, across(h)]

    def basis_x(place, side, h):
        ref = out_ref.at[place * 2 + side, core, :, across(h)]
        return pltpu.make_async_remote_copy(
            src_ref=ref, dst_ref=ref, send_sem=bx_send.at[place, h],
            recv_sem=bx_recv.at[place, h], device_id=to_x, device_id_type=MESH)

    def basis_core(at, who, h):
        ref = out_ref.at[at, who, :, across(h)]
        return pltpu.make_async_remote_copy(
            src_ref=ref, dst_ref=ref, send_sem=bc_send.at[at, h],
            recv_sem=bc_recv.at[at, h], device_id=to_core, device_id_type=MESH)

    def basis_begin(h):
        y_copy(h).wait_recv()
        both = both_cores(run, h) + y_in[:, across(h)].astype(jnp.float32)
        out_ref[tm, core, :, across(h)] = both.astype(jnp.bfloat16)

    def basis_pair(place, h):
        ref = out_ref.at[place * 2 + 1 - x, core, :, across(h)]
        return pltpu.make_async_remote_copy(
            src_ref=ref, dst_ref=ref, send_sem=bz_send.at[h], recv_sem=bz_recv.at[h],
            device_id=to_pair, device_id_type=MESH)

    def basis_ready(place, h):
        unless_by_pair(place, h, lambda: basis_x(place, x, h).start(), late)
        basis_core(place * 2 + x, core, h).start()

    def basis_to_pair():
        for h in late:
            basis_x(z, 1 - x, h).wait_recv()
            basis_pair(z, h).start()
            basis_core(z * 2 + 1 - x, core, h).start()

    basis_sends = line_gather(
        n_z, z, pieces, basis_slot, to_up, to_down, basis_begin, basis_ready, basis_to_pair,
        (b_up, b_down, b_recv))
    for turn, place in enumerate((z, 2 - far, 3 - 3 * far, pair)):
        for h in pieces:
            if turn == 0 and h in late:
                continue
            if turn == 3 and h in late:
                basis_pair(place, h).wait_recv()
            else:
                basis_x(place, 1 - x, h).wait_recv()
            basis_core(place * 2 + 1 - x, core, h).start()
    for h in pieces:
        for at in range(n_time):
            basis_core(at, 1 - core, h).wait_recv()
    frame_copy(run).wait_send()
    for k in chunks:
        for place in range(n_z):
            unless_by_pair(place, k, lambda: panel_x(place, x, k).wait_send())
    for k in by_pair:
        panel_pair(z, k).wait_send()
    panel_sends()
    basis_sends()
    for h in late:
        basis_pair(z, h).wait_send()
    for h in pieces:
        core_copy(h).wait_send()
        y_copy(h).wait_send()
        for place in range(n_z):
            unless_by_pair(place, h, lambda: basis_x(place, x, h).wait_send(), late)
        for at in range(n_time):
            basis_core(at, core, h).wait_send()


def gathered_basis(frames, low, high, n_time):
    t_local, features = frames.shape
    width = 2 * low.shape[0] * n_time
    n_z = n_time // 2
    half = t_local // 2
    dma = pltpu.SemaphoreType.DMA
    vmem = pltpu.VMEM
    flops = 2 * t_local * features * width
    return pl.pallas_call(
        functools.partial(kernel, n_time),
        out_shape=jax.ShapeDtypeStruct((n_time, 2, half, width), jnp.bfloat16),
        in_specs=[pl.BlockSpec(memory_space=pl.ANY)] * 3,
        out_specs=pl.BlockSpec(memory_space=pltpu.VMEM),
        scratch_shapes=[
            vmem((2, t_local, features // 2), jnp.bfloat16),
            vmem((2, n_time, low.shape[0], features // 2), jnp.bfloat16),
            vmem((2 * t_local, width), jnp.float32),
            vmem((2, 2, half, width), jnp.bfloat16),
            vmem((2, half, width), jnp.bfloat16),
            vmem((half, width), jnp.bfloat16),
            vmem((half, width), jnp.bfloat16),
            dma((3,)), dma((1,)), dma((1,)),
            *[dma((n_z, N_CHUNK))] * 5, dma((N_CHUNK,)), dma((N_CHUNK,)),
            *[dma((N_PIECE,))] * 4,
            *[dma((n_z, N_PIECE))] * 5, *[dma((n_time, N_PIECE))] * 2, *[dma((N_PIECE,))] * 2,
        ],
        compiler_params=pltpu.CompilerParams(
            collective_id=0, has_side_effects=True, vmem_limit_bytes=56 * 2**20),
        cost_estimate=pl.CostEstimate(flops=flops, bytes_accessed=16 * 2**20, transcendentals=0),
    )(frames, low, high)


def local(frames, panel_low, panel_high, lags, seg_lengths, ridge):
    t_local = frames.shape[1]
    n_time = lax.axis_size("tm")
    tm, core, run = lax.axis_index("tm"), lax.axis_index("feat"), lax.axis_index("rep")
    basis = gathered_basis(frames[0], panel_low.T, panel_high.T, n_time)
    width = basis.shape[-1]
    total = t_local * n_time
    basis = basis.reshape(total, width)
    rows = width // (n_time * 2)
    lag_most = t_local // 4
    lag_now = lags[0]
    positions = jnp.arange(total, dtype=jnp.int32)
    seg_ends = jnp.cumsum(seg_lengths[0])
    end_of = jnp.min(
        jnp.where(seg_ends[None, :] > positions[:, None], seg_ends[None, :], total), axis=1
    )
    keep = (positions + lag_now < end_of).astype(jnp.bfloat16)

    def later(values):
        spare = jnp.zeros((lag_most,) + values.shape[1:], values.dtype)
        return lax.dynamic_slice_in_dim(
            jnp.concatenate([spare, values], axis=0), lag_most - lag_now, total, 0)

    later_keep = later(keep)
    first = (tm * 2 + core) * rows
    own = lax.dynamic_slice(basis, (0, first), (total, rows))
    masked = own * keep[:, None]
    left = jnp.concatenate([masked, later(masked), own * later_keep[:, None]], axis=1)
    terms = jnp.einsum("ta,tj->aj", left, basis, preferred_element_type=jnp.float32)
    terms = terms.reshape(3, 2, rows // 2, width)
    variance = jnp.sum(
        jnp.square(basis.astype(jnp.float32)) * later_keep.astype(jnp.float32)[:, None], axis=0,
        keepdims=True)
    theirs = lax.dynamic_index_in_dim(terms, 1 - run, 1, keepdims=False).reshape(-1, width)
    mine = lax.dynamic_index_in_dim(terms, run, 1, keepdims=False)
    swap = [(0, 1), (1, 0)]
    received = lax.ppermute(theirs, "rep", swap)
    other_variance = lax.ppermute(variance, "rep", swap)
    inverse_count = 1.0 / (total * 2)
    cov_rows = (mine + received.reshape(mine.shape)) * inverse_count
    diag_lagged = (variance + other_variance)[0] * inverse_count
    return finish(cov_rows, diag_lagged, ridge)


def solution(mesh):
    in_specs = (
        P("rep", "tm", "feat"),
        P("feat", "tm"),
        P("feat", "tm"),
        P("rep"),
        P("rep", None),
        P(),
    )
    out_specs = (P(None, ("tm", "feat", "rep"), None), P(("tm", "feat", "rep"), None))
    shape = dict(mesh.shape)
    paired = shape["feat"] == 2 and shape["rep"] == 2 and shape["tm"] == 8
    body = local if paired else local_general
    return jax.shard_map(body, mesh=mesh, in_specs=in_specs, out_specs=out_specs, check_vma=False)
```

```python
import functools
import jax
import jax.numpy as jnp
from jax import lax
from jax.experimental import pallas as pl
from jax.experimental.pallas import tpu as pltpu
from jax.sharding import PartitionSpec as P

MESH = pl.DeviceIdType.MESH
N_CHUNK = 16
N_PIECE = 4
TILE = 1024


def passed_along(shard, axis, by):
    length = lax.axis_size(axis)
    pairs = [(i, i + by) for i in range(length) if 0 <= i + by < length]
    return lax.ppermute(shard, axis, pairs)


def local_general(frames, panel_low, panel_high, lags, seg_lengths, ridge):
    local_frames = frames[0]
    t_local = local_frames.shape[0]
    lag_most = t_local // 4
    n_time = lax.axis_size("tm")
    n_feature = lax.axis_size("feat")
    n_replica = lax.axis_size("rep")
    panel_cols = panel_low.shape[1] * n_time
    basis_width = 2 * panel_cols
    per_device = basis_width // (n_time * n_feature * n_replica)
    time_index = lax.axis_index("tm")
    feature_index = lax.axis_index("feat")
    replica_index = lax.axis_index("rep")
    stacked = jnp.stack([panel_low, panel_high], axis=0)
    partial_sum = jnp.einsum(
        "tf,pfk->tpk",
        local_frames,
        lax.all_gather(stacked, "tm", axis=2, tiled=True),
        preferred_element_type=jnp.float32,
    )
    partial_sum = partial_sum.reshape(local_frames.shape[0], basis_width)
    partial_rounded = partial_sum.astype(jnp.bfloat16)
    summed = lax.psum(partial_rounded, "feat").astype(jnp.float32).astype(jnp.bfloat16)
    next_basis = passed_along(summed[:lag_most], "tm", -1)
    extended = jnp.concatenate([summed, next_basis], axis=0)
    lag_now = lags[0]
    lagged = lax.dynamic_slice_in_dim(extended, lag_now, t_local, 0)
    frame_total = t_local * n_time
    positions = time_index * t_local + jnp.arange(t_local, dtype=jnp.int32)
    seg_ends = jnp.cumsum(seg_lengths[0])
    end_of = jnp.min(
        jnp.where(seg_ends[None, :] > positions[:, None], seg_ends[None, :], frame_total), axis=1
    )
    keep_mask = (positions + lag_now < end_of).astype(jnp.bfloat16)[:, None]
    masked = summed * keep_mask
    lag_masked = lagged * keep_mask

    def own_group(values):
        shaped = values.reshape(t_local, n_time, n_feature, n_replica * per_device)
        return lax.dynamic_index_in_dim(shaped, feature_index, 2, keepdims=False).reshape(
            t_local, -1
        )

    group_masked = own_group(masked)
    group_lagged = own_group(lag_masked)
    term_inst = jnp.einsum("ti,tj->ij", group_masked, summed, preferred_element_type=jnp.float32)
    term_cross = jnp.einsum("ti,tj->ij", group_masked, lagged, preferred_element_type=jnp.float32)
    term_lagged = jnp.einsum("ti,tj->ij", group_lagged, lagged, preferred_element_type=jnp.float32)
    row_block = lax.psum_scatter(
        jnp.stack([term_inst, term_cross, term_lagged], axis=1),
        ("tm", "rep"),
        scatter_dimension=0,
        tiled=True,
    )
    inverse_count = 1.0 / (frame_total * n_replica)
    cov_rows = jnp.transpose(row_block, (1, 0, 2)) * inverse_count
    local_var = jnp.sum(jnp.square(lag_masked.astype(jnp.float32)), axis=0)
    diag_lagged = lax.psum(local_var, ("tm", "rep")) * inverse_count
    return finish(cov_rows, diag_lagged, ridge)


def finish(cov_rows, diag_lagged, ridge):
    per_device, basis_width = cov_rows.shape[1:]
    device_linear = (
        lax.axis_index("tm") * lax.axis_size("feat") + lax.axis_index("feat")
    ) * lax.axis_size("rep") + lax.axis_index("rep")
    own_index = device_linear * per_device + jnp.arange(per_device, dtype=jnp.int32)
    selector = (jnp.arange(basis_width, dtype=jnp.int32)[None, :] == own_index[:, None]).astype(
        jnp.float32
    )
    diag_inst = jnp.sum(cov_rows[0] * selector, axis=1)
    inverse_lagged = 1.0 / (diag_lagged[:, None] + ridge[None, :])
    weighted = jnp.dot(
        jnp.square(cov_rows[1]),
        inverse_lagged,
        precision=lax.Precision.HIGHEST,
        preferred_element_type=jnp.float32,
    )
    scores = weighted / (diag_inst[:, None] + ridge[None, :])
    return (cov_rows, scores)


def line_gather(n_z, z, chunks, slot, send_up, send_down, begin, ready, at_end, sems):
    up_sem, down_sem, recv_sem = sems

    def copy(place, k, sem, target):
        return pltpu.make_async_remote_copy(
            src_ref=slot(place, k), dst_ref=slot(place, k), send_sem=sem.at[place, k],
            recv_sem=recv_sem.at[place, k], device_id=target, device_id_type=MESH)

    for k in chunks:
        begin(k)

        @pl.when(z + 1 < n_z)
        def _():
            copy(z, k, up_sem, send_up).start()

        @pl.when(z > 0)
        def _():
            copy(z, k, down_sem, send_down).start()

        ready(z, k)
    for step in range(1, n_z):
        for k in chunks:
            @pl.when(z - step >= 0)
            def _():
                place = z - step
                copy(place, k, up_sem, send_up).wait_recv()

                @pl.when(z + 1 < n_z)
                def _():
                    copy(place, k, up_sem, send_up).start()

                ready(place, k)

            @pl.when(z + step < n_z)
            def _():
                place = z + step
                copy(place, k, down_sem, send_down).wait_recv()

                @pl.when(z > 0)
                def _():
                    copy(place, k, down_sem, send_down).start()

                ready(place, k)

    at_end()

    def finish_sends():
        for place in range(n_z):
            for k in chunks:
                @pl.when(jnp.logical_and(z + 1 < n_z, place <= z))
                def _():
                    copy(place, k, up_sem, send_up).wait_send()

                @pl.when(jnp.logical_and(z > 0, place >= z))
                def _():
                    copy(place, k, down_sem, send_down).wait_send()

    return finish_sends


def kernel(n_time, frames_ref, low_ref, high_ref, out_ref, all_frames, all_panels, total, part, other,
           y_out, y_in, local_sem, f_send, f_recv, p_up, p_down, p_recv, px_send, px_recv,
           pz_send, pz_recv, c_send, c_recv, y_send, y_recv,
           b_up, b_down, b_recv, bx_send, bx_recv, bc_send, bc_recv, bz_send, bz_recv):
    n_z = n_time // 2
    tm, core, run = lax.axis_index("tm"), lax.axis_index("feat"), lax.axis_index("rep")
    z, x = tm // 2, tm % 2
    pair = z + 1 - 2 * (z % 2)
    to_up = (jnp.minimum(tm + 2, n_time - 2 + x), core, run)
    to_down = (jnp.maximum(tm - 2, x), core, run)
    to_pair = (pair * 2 + x, core, run)
    to_x = (z * 2 + (1 - x), core, run)
    to_y = (tm, core, 1 - run)
    to_core = (tm, 1 - core, run)
    features = all_frames.shape[2]
    cut = features // (N_CHUNK // 2)
    chunks = range(N_CHUNK)
    by_pair = range(N_CHUNK // 2, N_CHUNK)

    own_lanes = pl.ds(pl.multiple_of(run * features, features), features)
    their_lanes = pl.ds(pl.multiple_of((1 - run) * features, features), features)
    own_low = pltpu.make_async_copy(low_ref.at[:, own_lanes], all_panels.at[0, tm], local_sem.at[0])
    own_high = pltpu.make_async_copy(high_ref.at[:, own_lanes], all_panels.at[1, tm], local_sem.at[1])
    own_frames = pltpu.make_async_copy(
        frames_ref.at[:, own_lanes], all_frames.at[run], local_sem.at[2])
    own_low.start()
    own_high.start()
    own_frames.start()

    barrier = pltpu.get_barrier_semaphore()

    @pl.when(z + 1 < n_z)
    def _():
        pl.semaphore_signal(barrier, inc=1, device_id=to_up, device_id_type=MESH)

    @pl.when(z > 0)
    def _():
        pl.semaphore_signal(barrier, inc=1, device_id=to_down, device_id_type=MESH)

    for target in (to_x, to_y, to_core):
        pl.semaphore_signal(barrier, inc=1, device_id=target, device_id_type=MESH)

    @pl.when(jnp.logical_or(z == 0, z == n_z - 1))
    def _():
        pl.semaphore_wait(barrier, 4)

    @pl.when(jnp.logical_and(z > 0, z < n_z - 1))
    def _():
        pl.semaphore_wait(barrier, 5)

    def frame_copy(slot_run):
        return pltpu.make_async_remote_copy(
            src_ref=frames_ref.at[:, their_lanes], dst_ref=all_frames.at[slot_run],
            send_sem=f_send.at[0], recv_sem=f_recv.at[0], device_id=to_y, device_id_type=MESH)

    def panel_ref(place, side, k):
        return all_panels.at[
            k // (N_CHUNK // 2), place * 2 + side, :, pl.ds(k % (N_CHUNK // 2) * cut, cut)]

    def panel_slot(place, k):
        return panel_ref(place, x, k)

    def panel_x(place, side, k):
        ref = panel_ref(place, side, k)
        return pltpu.make_async_remote_copy(
            src_ref=ref, dst_ref=ref, send_sem=px_send.at[place, k],
            recv_sem=px_recv.at[place, k], device_id=to_x, device_id_type=MESH)

    def panel_pair(place, k):
        ref = panel_ref(place, 1 - x, k)
        return pltpu.make_async_remote_copy(
            src_ref=ref, dst_ref=ref, send_sem=pz_send.at[k], recv_sem=pz_recv.at[k],
            device_id=to_pair, device_id_type=MESH)

    def unless_by_pair(place, k, act, passed=by_pair):
        if k in passed:
            pl.when(place != pair)(act)
        else:
            act()

    def panel_begin(k):
        if k == 0:
            own_low.wait()
        if k == N_CHUNK // 2:
            own_high.wait()

    def panel_ready(place, k):
        unless_by_pair(place, k, lambda: panel_x(place, x, k).start())

    def pass_to_pair():
        for k in by_pair:
            panel_x(z, 1 - x, k).wait_recv()
            panel_pair(z, k).start()

    frame_copy(run).start()
    panel_sends = line_gather(
        n_z, z, chunks, panel_slot, to_up, to_down, panel_begin, panel_ready, pass_to_pair,
        (p_up, p_down, p_recv))
    own_frames.wait()
    frame_copy(1 - run).wait_recv()
    far = z // 2
    rows, columns = total.shape
    block = all_panels.shape[2] * 2
    for turn, place in enumerate((z, 2 - far, 3 - 3 * far, pair)):
        for k in chunks:
            if turn == 0 and k in by_pair:
                continue
            if turn == 3 and k in by_pair:
                panel_pair(place, k).wait_recv()
            else:
                panel_x(place, 1 - x, k).wait_recv()

        def term(i, so_far):
            at = pl.ds(pl.multiple_of(i * TILE, TILE), TILE)
            left = all_frames[:, :, at].reshape(rows, TILE)
            right = all_panels[:, pl.ds(place * 2, 2), :, at].reshape(2 * block, TILE)
            return so_far + lax.dot_general(
                left, right, (((1,), (1,)), ((), ())), preferred_element_type=jnp.float32)

        result = lax.fori_loop(
            0, features // TILE, term, jnp.zeros((rows, 2 * block), jnp.float32))
        for panel in range(2):
            at = pl.ds(pl.multiple_of(panel * (columns // 2) + place * block, block), block)
            total[:, at] = result[:, panel * block:(panel + 1) * block]
            part[:, :, :, at] = result[:, panel * block:(panel + 1) * block].astype(
                jnp.bfloat16).reshape(2, 2, rows // 4, block)

    half = rows // 4
    wide = columns // N_PIECE
    pieces = range(N_PIECE)
    late = range(N_PIECE // 2, N_PIECE)
    own_rows = pl.multiple_of(core * half, half)

    def across(h):
        return pl.ds(h * wide, wide)

    def core_copy(h):
        return pltpu.make_async_remote_copy(
            src_ref=part.at[:, 1 - core, :, across(h)], dst_ref=other.at[:, :, across(h)],
            send_sem=c_send.at[h], recv_sem=c_recv.at[h], device_id=to_core, device_id_type=MESH)

    def y_copy(h):
        return pltpu.make_async_remote_copy(
            src_ref=y_out.at[:, across(h)], dst_ref=y_in.at[:, across(h)],
            send_sem=y_send.at[h], recv_sem=y_recv.at[h], device_id=to_y, device_id_type=MESH)

    def both_cores(which, h):
        first = pl.multiple_of(which * 2 * half + own_rows, half)
        return total[pl.ds(first, half), across(h)] + other[which, :, across(h)].astype(jnp.float32)

    for h in pieces:
        core_copy(h).start()
    for h in pieces:
        core_copy(h).wait_recv()
        y_out[:, across(h)] = both_cores(1 - run, h).astype(jnp.bfloat16)
        y_copy(h).start()

    def basis_slot(place, h):
        return out_ref.at[place * 2 + x, core, :, across(h)]

    def basis_x(place, side, h):
        ref = out_ref.at[place * 2 + side, core, :, across(h)]
        return pltpu.make_async_remote_copy(
            src_ref=ref, dst_ref=ref, send_sem=bx_send.at[place, h],
            recv_sem=bx_recv.at[place, h], device_id=to_x, device_id_type=MESH)

    def basis_core(at, who, h):
        ref = out_ref.at[at, who, :, across(h)]
        return pltpu.make_async_remote_copy(
            src_ref=ref, dst_ref=ref, send_sem=bc_send.at[at, h],
            recv_sem=bc_recv.at[at, h], device_id=to_core, device_id_type=MESH)

    def basis_begin(h):
        y_copy(h).wait_recv()
        both = both_cores(run, h) + y_in[:, across(h)].astype(jnp.float32)
        out_ref[tm, core, :, across(h)] = both.astype(jnp.bfloat16)

    def basis_pair(place, h):
        ref = out_ref.at[place * 2 + 1 - x, core, :, across(h)]
        return pltpu.make_async_remote_copy(
            src_ref=ref, dst_ref=ref, send_sem=bz_send.at[h], recv_sem=bz_recv.at[h],
            device_id=to_pair, device_id_type=MESH)

    def basis_ready(place, h):
        unless_by_pair(place, h, lambda: basis_x(place, x, h).start(), late)
        basis_core(place * 2 + x, core, h).start()

    def basis_to_pair():
        for h in late:
            basis_x(z, 1 - x, h).wait_recv()
            basis_pair(z, h).start()
            basis_core(z * 2 + 1 - x, core, h).start()

    basis_sends = line_gather(
        n_z, z, pieces, basis_slot, to_up, to_down, basis_begin, basis_ready, basis_to_pair,
        (b_up, b_down, b_recv))
    for turn, place in enumerate((z, 2 - far, 3 - 3 * far, pair)):
        for h in pieces:
            if turn == 0 and h in late:
                continue
            if turn == 3 and h in late:
                basis_pair(place, h).wait_recv()
            else:
                basis_x(place, 1 - x, h).wait_recv()
            basis_core(place * 2 + 1 - x, core, h).start()
    for h in pieces:
        for at in range(n_time):
            basis_core(at, 1 - core, h).wait_recv()
    frame_copy(run).wait_send()
    for k in chunks:
        for place in range(n_z):
            unless_by_pair(place, k, lambda: panel_x(place, x, k).wait_send())
    for k in by_pair:
        panel_pair(z, k).wait_send()
    panel_sends()
    basis_sends()
    for h in late:
        basis_pair(z, h).wait_send()
    for h in pieces:
        core_copy(h).wait_send()
        y_copy(h).wait_send()
        for place in range(n_z):
            unless_by_pair(place, h, lambda: basis_x(place, x, h).wait_send(), late)
        for at in range(n_time):
            basis_core(at, core, h).wait_send()


def gathered_basis(frames, low, high, n_time):
    t_local, features = frames.shape
    width = 2 * low.shape[0] * n_time
    n_z = n_time // 2
    half = t_local // 2
    dma = pltpu.SemaphoreType.DMA
    vmem = pltpu.VMEM
    flops = 2 * t_local * features * width
    return pl.pallas_call(
        functools.partial(kernel, n_time),
        out_shape=jax.ShapeDtypeStruct((n_time, 2, half, width), jnp.bfloat16),
        in_specs=[pl.BlockSpec(memory_space=pl.ANY)] * 3,
        out_specs=pl.BlockSpec(memory_space=pltpu.VMEM),
        scratch_shapes=[
            vmem((2, t_local, features // 2), jnp.bfloat16),
            vmem((2, n_time, low.shape[0], features // 2), jnp.bfloat16),
            vmem((2 * t_local, width), jnp.float32),
            vmem((2, 2, half, width), jnp.bfloat16),
            vmem((2, half, width), jnp.bfloat16),
            vmem((half, width), jnp.bfloat16),
            vmem((half, width), jnp.bfloat16),
            dma((3,)), dma((1,)), dma((1,)),
            *[dma((n_z, N_CHUNK))] * 5, dma((N_CHUNK,)), dma((N_CHUNK,)),
            *[dma((N_PIECE,))] * 4,
            *[dma((n_z, N_PIECE))] * 5, *[dma((n_time, N_PIECE))] * 2, *[dma((N_PIECE,))] * 2,
        ],
        compiler_params=pltpu.CompilerParams(
            collective_id=0, has_side_effects=True, vmem_limit_bytes=56 * 2**20),
        cost_estimate=pl.CostEstimate(flops=flops, bytes_accessed=16 * 2**20, transcendentals=0),
    )(frames, low, high)


def local(frames, panel_low, panel_high, lags, seg_lengths, ridge):
    t_local = frames.shape[1]
    n_time = lax.axis_size("tm")
    tm, core, run = lax.axis_index("tm"), lax.axis_index("feat"), lax.axis_index("rep")
    basis = gathered_basis(frames[0], panel_low.T, panel_high.T, n_time)
    width = basis.shape[-1]
    total = t_local * n_time
    basis = basis.reshape(total, width)
    rows = width // (n_time * 2)
    lag_most = t_local // 4
    lag_now = lags[0]
    positions = jnp.arange(total, dtype=jnp.int32)
    seg_ends = jnp.cumsum(seg_lengths[0])
    end_of = jnp.min(
        jnp.where(seg_ends[None, :] > positions[:, None], seg_ends[None, :], total), axis=1
    )
    keep = (positions + lag_now < end_of).astype(jnp.bfloat16)

    def later(values):
        spare = jnp.zeros((lag_most,) + values.shape[1:], values.dtype)
        return lax.dynamic_slice_in_dim(
            jnp.concatenate([spare, values], axis=0), lag_most - lag_now, total, 0)

    later_keep = later(keep)
    first = (tm * 2 + core) * rows
    own = lax.dynamic_slice(basis, (0, first), (total, rows))
    masked = own * keep[:, None]
    left = jnp.concatenate([masked, later(masked), own * later_keep[:, None]], axis=1)
    terms = jnp.einsum("ta,tj->aj", left, basis, preferred_element_type=jnp.float32)
    terms = terms.reshape(3, 2, rows // 2, width)
    variance = jnp.sum(
        jnp.square(basis.astype(jnp.float32)) * later_keep.astype(jnp.float32)[:, None], axis=0,
        keepdims=True)
    theirs = lax.dynamic_index_in_dim(terms, 1 - run, 1, keepdims=False).reshape(-1, width)
    mine = lax.dynamic_index_in_dim(terms, run, 1, keepdims=False)
    swap = [(0, 1), (1, 0)]
    received = lax.ppermute(theirs, "rep", swap)
    other_variance = lax.ppermute(variance, "rep", swap)
    inverse_count = 1.0 / (total * 2)
    cov_rows = (mine + received.reshape(mine.shape)) * inverse_count
    diag_lagged = (variance + other_variance)[0] * inverse_count
    return finish(cov_rows, diag_lagged, ridge)


def solution(mesh):
    in_specs = (
        P("rep", "tm", "feat"),
        P("feat", "tm"),
        P("feat", "tm"),
        P("rep"),
        P("rep", None),
        P(),
    )
    out_specs = (P(None, ("tm", "feat", "rep"), None), P(("tm", "feat", "rep"), None))
    shape = dict(mesh.shape)
    paired = shape["feat"] == 2 and shape["rep"] == 2 and shape["tm"] == 8
    body = local if paired else local_general
    return jax.shard_map(body, mesh=mesh, in_specs=in_specs, out_specs=out_specs, check_vma=False)
```
